32 devices in a mesh: groups: 2 (over x), row: 8 (over z, y), col: 2 (over core).
Axes of the slice: x: 2, y: 2, z: 4, core: 2. Of those that a mesh axis runs over, the one named last changes fastest.
Arguments:
- d_blocks: float32 [16, 2, 6, 128, 128], P(('groups', 'row'), 'col'), parts along dimension 0
- d_index: int32 [16, 2, 6, 2], P(('groups', 'row'), 'col'), parts along dimension 0, may hold values from 0 to 31, as said below
- row_perm: int32 [64], P('groups'), parts along dimension 0, may hold values from 0 to 31, as said below
- ks_blocks: float32 [16, 4, 10, 128, 128], P(('groups', 'row'), 'col'), parts along dimension 0
- ks_index: int32 [16, 4, 10], P(('groups', 'row'), 'col'), parts along dimension 0, may hold values from 0 to 15, as said below
- c_index: int32 [16, 2, 16], P(('groups', 'row'), 'col'), parts along dimension 0, may hold values from 0 to 63, as said below
Outputs:
- c_blocks: float32 [16, 2, 16, 128, 128], P(('groups', 'row'), 'col'), parts along dimension 0
The draws below stay inside these ranges and needn't reach their ends.
There are 2 independent parts, one for each index of `groups`. The reference program is written for one: setup_inputs(seed, part) draws one part's arguments, and reference() takes and returns one part's arrays. A program takes and returns all parts, laid end to end along the dimension named above; each array names one. Nothing has to cross between parts.
Inputs may be any that keep to these rules, and one draw needn't show every extreme that they name: `d_index`: no density block is listed twice within a column half; at most 2 blocks of one device, and at most 12 blocks of one column half, fall into one grid row panel (block rows whose row_perm values share one quotient by 4); both bounds are reached. `row_perm`: A permutation of the block rows. `ks_index`: positions within one window block are distinct. `c_index`: positions on one device are distinct.
All inputs are finite; a program needn't handle non-finite values.
Results may differ from the reference program's by a relative error of at most 0.0003.
Values sent between devices are 32-bit elements; how exact they have to be, the bound alone decides.
No kernel may reach another device: no remote copies, remote signals or barrier semaphores. Data moves between devices by JAX's collectives and lax.ppermute only.
A program may use at most 128 MiB of HBM per device.

```python
import math
import jax
import jax.numpy as jnp
from jax import lax

BS = 128
BR = 4
NB = 32
NBC = 16
STOPS = 4
KSS = 10
OSLOT = 6
CSLOT = 16
N_ROW = 8
N_COL = 2


def density_layout(key):
    key = jax.random.fold_in(key, 11)
    perm_key, col_key = jax.random.split(key)
    row_perm = jax.random.permutation(perm_key, NB).astype(jnp.int32)
    inverse = jnp.argsort(row_perm).astype(jnp.int32)
    half_cols = NB // N_COL

    def one_half(half_key):
        keys = jax.random.split(half_key, 4)
        dest_perm = jax.random.permutation(keys[0], N_ROW)
        owner_perm = jax.random.permutation(keys[1], N_ROW)
        heavy = dest_perm < N_ROW // 4
        within = jnp.where(heavy, dest_perm, dest_perm - N_ROW // 4)
        parity = ((owner_perm[:, None] + within[None, :]) % 2 == 0).astype(jnp.int32)
        counts = jnp.where(heavy[None, :], 1 + parity, parity)
        before = jnp.cumsum(counts, axis=0) - counts
        running = jnp.cumsum(counts, axis=1)
        slots = jnp.arange(OSLOT)
        target = jnp.sum((running[:, None, :] <= slots[None, :, None]).astype(jnp.int32), axis=2)
        start = jnp.take_along_axis(running - counts, target, axis=1)
        arrival = jnp.take_along_axis(before, target, axis=1) + slots[None, :] - start
        places = jax.vmap(lambda sub_key: jax.random.permutation(sub_key, BR * half_cols))(jax.random.split(keys[2], N_ROW))
        place = places[target, arrival]
        inner_row = place // half_cols
        column = place % half_cols
        block_row = inverse[target * BR + inner_row]
        shuffle = jax.vmap(lambda sub_key: jax.random.permutation(sub_key, OSLOT))(jax.random.split(keys[3], N_ROW))
        block_row = jnp.take_along_axis(block_row, shuffle, axis=1)
        column = jnp.take_along_axis(column, shuffle, axis=1)
        occupied = jnp.zeros((N_ROW, BR, half_cols), jnp.int32).at[target, inner_row, column].set(1)
        return (jnp.stack([block_row, column], axis=-1).astype(jnp.int32), occupied)
    lists, occupied = jax.vmap(one_half)(jax.random.split(col_key, N_COL))
    return (row_perm, jnp.transpose(lists, (1, 0, 2, 3)), occupied)


def ks_layout(key):
    key = jax.random.fold_in(key, 22)
    keys = jax.random.split(key, N_ROW * STOPS)
    places = jax.vmap(lambda sub_key: jax.random.permutation(sub_key, BR * BR)[:KSS])(keys)
    return places.reshape(N_ROW, STOPS, KSS).astype(jnp.int32)


def block_scales(key, lead):
    flag_key, small_key, large_key = jax.random.split(key, 3)
    faint = jax.random.bernoulli(flag_key, 0.3, lead)
    small = jax.random.uniform(small_key, lead, jnp.float32, 0.1, 0.2)
    large = jnp.exp(jax.random.uniform(large_key, lead, jnp.float32, math.log(0.7), math.log(1.4)))
    return jnp.where(faint, small, large)


def draw_row_perm(key, part):
    return density_layout(key)[0]


def draw_d_index(key, part):
    return density_layout(key)[1]


def draw_ks_index(key, part):
    return ks_layout(key)


def draw_c_index(key, part):
    row_perm, lists, occupied = density_layout(key)
    ks_places = ks_layout(key)
    key = jax.random.fold_in(key, 33)
    present = jnp.any(ks_places[..., None] == jnp.arange(BR * BR)[None, None, None, :], axis=2)
    present = present.reshape(N_ROW, STOPS, BR, BR).astype(jnp.int32)
    panels = (jnp.arange(N_ROW)[:, None] + jnp.arange(STOPS)[None, :]) % N_ROW
    window = occupied[:, panels]
    hits = (jnp.einsum('rsik,crskj->rcij', present, window) > 0).astype(jnp.int32)
    hits = hits.reshape(N_ROW, N_COL, BR * NBC)
    orders = jax.vmap(lambda sub_key: jax.random.permutation(sub_key, BR * NBC))(jax.random.split(key, N_ROW * N_COL))
    scores = hits * (BR * NBC) + orders.reshape(N_ROW, N_COL, BR * NBC)
    chosen = lax.top_k(scores, CSLOT)[1]
    return chosen.astype(jnp.int32)


def draw_d_blocks(key, part):
    key = jax.random.fold_in(key, 44)
    entry_key, scale_key = jax.random.split(key)
    shape = (N_ROW, N_COL, OSLOT, BS, BS)
    entries = jax.random.truncated_normal(entry_key, -4.0, 4.0, shape, jnp.float32)
    return entries * block_scales(scale_key, shape[:3])[..., None, None]


def draw_ks_blocks(key, part):
    key = jax.random.fold_in(key, 55)
    entry_key, scale_key = jax.random.split(key)
    shape = (N_ROW, STOPS, KSS, BS, BS)
    entries = jax.random.truncated_normal(entry_key, -4.0, 4.0, shape, jnp.float32)
    return entries * (block_scales(scale_key, shape[:3]) / math.sqrt(BS))[..., None, None]


def setup_inputs(seed: int = 0, part: int = 0) -> dict:
    key_list = jax.random.split(jax.random.key(seed), 7)
    own_keys = jax.random.split(jax.random.fold_in(key_list[6], part), 7)
    d_blocks = draw_d_blocks(jax.random.fold_in(jax.random.fold_in(key_list[6], part), 71), part)
    d_index = draw_d_index(jax.random.fold_in(jax.random.fold_in(key_list[6], part), 71), part)
    row_perm = draw_row_perm(jax.random.fold_in(jax.random.fold_in(key_list[6], part), 71), part)
    ks_blocks = draw_ks_blocks(jax.random.fold_in(jax.random.fold_in(key_list[6], part), 71), part)
    ks_index = draw_ks_index(jax.random.fold_in(jax.random.fold_in(key_list[6], part), 71), part)
    c_index = draw_c_index(jax.random.fold_in(jax.random.fold_in(key_list[6], part), 71), part)
    return {"d_blocks": d_blocks, "d_index": d_index, "row_perm": row_perm, "ks_blocks": ks_blocks, "ks_index": ks_index, "c_index": c_index}


FILTER = 0.055

def window_blocks(slots, places):
    onehot = (places[:, None] == jnp.arange(BR * BR)[None, :]).astype(jnp.float32)
    return jnp.einsum('qp,qxy->pxy', onehot, slots, precision=lax.Precision.HIGHEST)

def block_norms(blocks):
    return jnp.sqrt(lax.optimization_barrier(jnp.sum(blocks * blocks, axis=(-2, -1))))

def reference(d_blocks, d_index, row_perm, ks_blocks, ks_index, c_index):
    limit = FILTER * BS * math.sqrt(BS)
    shape = (N_ROW, N_COL, OSLOT)
    flat_owner = jnp.broadcast_to(jnp.arange(N_ROW)[:, None, None] * OSLOT + jnp.arange(OSLOT)[None, None, :], shape).astype(jnp.int32)
    halves = jnp.broadcast_to(jnp.arange(N_COL)[None, :, None], shape).astype(jnp.int32)
    grid_position = row_perm[d_index[..., 0]]
    locator = jnp.full((N_COL, NB, NBC), -1, jnp.int32).at[halves, grid_position, d_index[..., 1]].set(flat_owner)
    density_norms = block_norms(d_blocks)
    inner_rows = jnp.arange(BR)

    def device_product(device):
        panel_row = device // N_COL
        half = device % N_COL
        targets = c_index[panel_row, half]
        target_rows = targets // NBC
        target_cols = targets % NBC
        accumulated = jnp.zeros((CSLOT, BS, BS), jnp.float32)
        for station in range(STOPS):
            window = window_blocks(ks_blocks[panel_row, station], ks_index[panel_row, station])
            window_norms = block_norms(window)
            grid_rows = (panel_row + station) % (NB // BR) * BR + inner_rows
            located = locator[half][grid_rows[None, :], target_cols[:, None]]
            present_pair = located >= 0
            safe_slot = jnp.maximum(located, 0)
            owner = safe_slot // OSLOT
            owner_slot = safe_slot % OSLOT
            chosen = d_blocks[owner, half, owner_slot]
            chosen_norms = density_norms[owner, half, owner_slot]
            picked = target_rows[:, None] * BR + inner_rows[None, :]
            ks_pick = window[picked]
            ks_norms = window_norms[picked]
            retained = present_pair & (ks_norms * chosen_norms >= limit)
            masked = jnp.where(retained[..., None, None], ks_pick, 0.0)
            accumulated = accumulated + jnp.einsum('tkxy,tkyz->txz', masked, chosen, precision=lax.Precision.HIGHEST)
        return accumulated
    products = lax.map(device_product, jnp.arange(N_ROW * N_COL))
    return products.reshape(N_ROW, N_COL, CSLOT, BS, BS)
```

```python
import functools
import math

import jax
import jax.numpy as jnp
from jax import lax
from jax.experimental import pallas as pl
from jax.experimental.pallas import tpu as pltpu
from jax.sharding import PartitionSpec as P

BR = 4
CAPX = 2


FILTER = 0.055
UNROLL = 4
VMEM_GRANT = 8 * 1024 * 1024


def passed_along(shard, axis, by):
    size = lax.axis_size(axis)
    return lax.ppermute(shard, axis, [(i, (i + by) % size) for i in range(size)])


def window_blocks(slots, places):
    onehot = (places[:, None] == jnp.arange(BR * BR)[None, :]).astype(jnp.float32)
    return jnp.einsum("qp,qxy->pxy", onehot, slots, precision=lax.Precision.HIGHEST)


def block_norms(blocks):
    return jnp.sqrt(jnp.sum(blocks * blocks, axis=(-2, -1)))


def stop_product(density_panel, panel_labels, panel_norms, ks_slots, ks_places, targets, half_cols):
    block_size = density_panel.shape[-1]
    limit = FILTER * block_size * math.sqrt(block_size)
    window = window_blocks(ks_slots, ks_places)
    window_norms = block_norms(window)
    target_rows = targets // half_cols
    target_cols = targets % half_cols
    slot_range = jnp.arange(density_panel.shape[0])
    inner_rows = jnp.arange(BR)
    matches = (panel_labels[None, None, :, 0] == inner_rows[None, :, None]) & (
        panel_labels[None, None, :, 1] == target_cols[:, None, None]
    )
    present_pair = jnp.any(matches, axis=2)
    where_slot = jnp.sum(matches.astype(jnp.int32) * slot_range[None, None, :], axis=2)
    chosen = density_panel[where_slot]
    chosen_norms = panel_norms[where_slot]
    picked = target_rows[:, None] * BR + inner_rows[None, :]
    ks_norms = window_norms[picked]
    retained = present_pair & (ks_norms * chosen_norms >= limit)
    masked = jnp.where(retained[..., None, None], window[picked], 0.0)
    return jnp.einsum("tkxy,tkyz->txz", masked, chosen, precision=lax.Precision.HIGHEST)


def panel_plan(d_blocks, d_index, row_perm, ks_blocks, ks_index, c_index):
    row_count = lax.axis_size("row")
    block_size = d_blocks.shape[-1]
    blocks = d_blocks.reshape(-1, block_size, block_size)
    slot_list = d_index.reshape(-1, 2)
    block_rows = row_perm.shape[0]
    half_cols = block_rows // lax.axis_size("col")
    capacity = 3 * row_count // 2
    position = jnp.sum(
        jnp.where(slot_list[:, 0:1] == jnp.arange(block_rows)[None, :], row_perm[None, :], 0),
        axis=1,
    )
    grid_panel = position // BR
    inner_row = position % BR
    onehot = (grid_panel[:, None] == jnp.arange(row_count)[None, :]).astype(jnp.int32)
    arrival_rank = jnp.sum((jnp.cumsum(onehot, axis=0) - onehot) * onehot, axis=1)
    send_slot = grid_panel * CAPX + arrival_rank
    outgoing = (
        jnp.zeros((row_count * CAPX, block_size, block_size), jnp.float32).at[send_slot].set(blocks)
    )
    outgoing = outgoing.reshape(row_count, CAPX, block_size, block_size)
    labels = (
        jnp.full((row_count * CAPX, 2), -1, jnp.int32)
        .at[send_slot]
        .set(jnp.stack([inner_row, slot_list[:, 1]], axis=1))
    )
    labels = labels.reshape(row_count, CAPX, 2)
    arrived, arrived_labels = (
        lax.all_to_all(outgoing, "row", split_axis=0, concat_axis=0, tiled=True),
        lax.all_to_all(labels, "row", split_axis=0, concat_axis=0, tiled=True),
    )
    arrived = arrived.reshape(-1, block_size, block_size)
    arrived_labels = arrived_labels.reshape(-1, 2)
    keep_order = jnp.argsort((arrived_labels[:, 0] < 0).astype(jnp.int32), stable=True)[:capacity]
    density_panel = arrived[keep_order]
    panel_labels = arrived_labels[keep_order]
    ks_all, ks_places = (
        lax.all_gather(ks_blocks, "col", axis=1, tiled=True),
        lax.all_gather(ks_index, "col", axis=1, tiled=True),
    )
    ks_all = ks_all[0]
    ks_places = ks_places[0]
    targets = c_index.reshape(-1)
    stop_count = ks_all.shape[0]
    panel_norms = block_norms(density_panel)
    accumulated = jnp.zeros((targets.shape[0], block_size, block_size), jnp.float32)
    for station in range(stop_count):
        accumulated = accumulated + stop_product(
            density_panel,
            panel_labels,
            panel_norms,
            ks_all[station],
            ks_places[station],
            targets,
            half_cols,
        )
        if station + 1 < stop_count:
            density_panel, panel_labels, panel_norms = passed_along(
                (density_panel, panel_labels, panel_norms), "row", -1
            )
    return accumulated.reshape(c_index.shape + (block_size, block_size))


def ring_order(count):
    return list(range(0, count, 2)) + list(range(1, count, 2))[::-1]


def split_bf16(x):
    high = x.astype(jnp.bfloat16)
    return high, (x - high.astype(jnp.float32)).astype(jnp.bfloat16)


def norm_of(x):
    columns = jnp.sum(x * x, axis=0, keepdims=True)
    return jnp.sqrt(jnp.sum(columns, axis=1, keepdims=True))


def in_vmem(x):
    return pltpu.with_memory_space_constraint(x, pltpu.VMEM)


SMEM_SPEC = pl.BlockSpec(memory_space=pltpu.SMEM)
VMEM_SPEC = pl.BlockSpec(memory_space=pltpu.VMEM)


def split_kernel(own_ref, twin_ref, parts_ref, norms_ref):
    count = own_ref.shape[0]
    for half, ref in enumerate((own_ref, twin_ref)):

        def one(q, _, half=half, ref=ref):
            block = ref[q]
            parts_ref[half * count + q] = jnp.concatenate(split_bf16(block), axis=1)
            norms_ref[half * count + q] = jnp.broadcast_to(norm_of(block), norms_ref.shape[1:])

        lax.fori_loop(0, count, one, None, unroll=4)


def split_ks(own, twin):
    count, block_size, _ = own.shape
    return pl.pallas_call(
        split_kernel,
        out_shape=(
            pltpu.VMEM((2 * count, block_size, 2 * block_size), jnp.bfloat16),
            pltpu.VMEM((2 * count, 1, block_size), jnp.float32),
        ),
        in_specs=[VMEM_SPEC] * 2,
        out_specs=(VMEM_SPEC,) * 2,
        compiler_params=pltpu.CompilerParams(vmem_limit_bytes=VMEM_GRANT),
    )(in_vmem(own), in_vmem(twin))


def product_kernel(config, *refs):
    row_count, stop_count, half_cols, limit, pieces, first = config
    perm_ref, own_place_ref, twin_place_ref, target_ref, parts_ref, norms_ref = refs[:6]
    chunk_refs = refs[6 : 6 + len(pieces)]
    rest = refs[6 + len(pieces) :]
    if first:
        c_ref = rest[0]
        rest = rest[1:]
    else:
        c_in_ref, c_ref = rest[:2]
        rest = rest[2:]
    target_at, ks_at, label, list_t, list_q, list_b, held, sems = rest
    block_size = c_ref.shape[-1]
    half_stops, present = own_place_ref.shape
    row, col = lax.axis_index("row"), lax.axis_index("col")

    copies = []
    for number, (blocks, _, labels) in enumerate(pieces):
        if labels is None:
            chunk_ref = chunk_refs[number]
            rows = pl.ds(blocks * block_size, chunk_ref.shape[0] - blocks * block_size)
            slot = len(copies)
            copies.append(pltpu.make_async_copy(chunk_ref.at[rows], label.at[slot], sems.at[slot]))
            copies[-1].start()

    for i in range(target_at.shape[0]):
        target_at[i] = -1
    for i in range(ks_at.shape[0]):
        ks_at[i] = -1
    for t in range(target_ref.shape[0]):
        target_at[target_ref[t]] = t
    for local in range(half_stops):
        own_base = (col * half_stops + local) * BR * BR
        twin_base = ((1 - col) * half_stops + local) * BR * BR
        for q in range(present):
            ks_at[own_base + own_place_ref[local, q]] = local * present + q
            ks_at[twin_base + twin_place_ref[local, q]] = (half_stops + local) * present + q
    if first:
        c_ref[...] = jnp.zeros_like(c_ref)
    else:
        c_ref[...] = c_in_ref[...]
    for copy in copies:
        copy.wait()

    slots = {}
    for number, (_, _, labels) in enumerate(pieces):
        if labels is None:
            slots[number] = len(slots)
    found = (jnp.int32(0), jnp.int32(0))
    for number, (blocks, offset, labels) in enumerate(pieces):
        chunk_ref = chunk_refs[number]
        slot = slots[number if labels is None else labels]

        def look(b, found, chunk_ref=chunk_ref, slot=slot, offset=offset):
            pairs, kept = found
            position = perm_ref[label[slot, offset + b, 0].astype(jnp.int32)]
            column = label[slot, offset + b, 1].astype(jnp.int32)
            behind = lax.div(position, BR) - row
            stop = jnp.where(behind < 0, behind + row_count, behind)
            in_window = stop < stop_count
            place = jnp.minimum(stop, stop_count - 1) * BR * BR + lax.rem(position, BR)
            before = pairs
            for i in range(BR):
                target = target_at[i * half_cols + column]
                ks = ks_at[place + i * BR]
                list_t[pairs] = target
                list_q[pairs] = ks
                list_b[pairs] = kept
                hit = (target >= 0) & (ks >= 0) & in_window
                pairs = pairs + hit.astype(jnp.int32)
            some = pairs > before

            @pl.when(some)
            def _():
                held[kept] = chunk_ref[pl.ds(pl.multiple_of(b * block_size, block_size), block_size), :]

            return pairs, kept + some.astype(jnp.int32)

        found = lax.fori_loop(0, blocks, look, found)
    pairs, _ = found
    for u in range(UNROLL):
        list_t[pairs + u] = 0
        list_q[pairs + u] = 0
        list_b[pairs + u] = 0

    def multiply(step, _):
        for u in range(UNROLL):
            at = step * UNROLL + u
            target, ks, slot = list_t[at], list_q[at], list_b[at]
            density = held[slot]
            bound = jnp.where(at < pairs, limit, jnp.inf)
            keep = norms_ref[ks] * norm_of(density) >= bound
            high, low = split_bf16(density)
            weights = jnp.concatenate(
                [
                    jnp.concatenate([high, low], axis=1),
                    jnp.concatenate([high, jnp.zeros_like(low)], axis=1),
                ],
                axis=0,
            )
            both = jnp.dot(parts_ref[ks], weights, preferred_element_type=jnp.float32)
            value = both[:, :block_size] + both[:, block_size:]
            c_ref[target] += jnp.where(keep, value, 0.0)

    lax.fori_loop(0, lax.div(pairs + UNROLL - 1, UNROLL), multiply, None)


def add_products(sizes, tables, parts, norms, accumulated, pieces, chunks, shape):
    block_size = shape[-1]
    limit = FILTER * block_size * math.sqrt(block_size)
    first = accumulated is None
    blocks = sum(piece[0] for piece in pieces)
    labelled = [n for n, piece in enumerate(pieces) if piece[2] is None]
    label_rows = chunks[labelled[0]].shape[0] - pieces[labelled[0]][0] * block_size
    operands = [*tables, in_vmem(parts), in_vmem(norms), *map(in_vmem, chunks)]
    in_specs = [SMEM_SPEC] * len(tables) + [VMEM_SPEC] * (2 + len(chunks))
    if not first:
        operands.append(in_vmem(accumulated))
        in_specs.append(VMEM_SPEC)
    longest = blocks * BR + 2 * UNROLL
    return pl.pallas_call(
        functools.partial(product_kernel, (*sizes, limit, pieces, first)),
        out_shape=pltpu.VMEM(shape, jnp.float32) if first else jax.ShapeDtypeStruct(shape, jnp.float32),
        in_specs=in_specs,
        out_specs=VMEM_SPEC,
        scratch_shapes=[
            pltpu.SMEM((BR * sizes[2],), jnp.int32),
            pltpu.SMEM((sizes[1] * BR * BR,), jnp.int32),
            pltpu.SMEM((len(labelled), label_rows, block_size), jnp.float32),
            pltpu.SMEM((longest,), jnp.int32),
            pltpu.SMEM((longest,), jnp.int32),
            pltpu.SMEM((longest,), jnp.int32),
            pltpu.VMEM((blocks, block_size, block_size), jnp.float32),
            pltpu.SemaphoreType.DMA((len(labelled),)),
        ],
        compiler_params=pltpu.CompilerParams(vmem_limit_bytes=VMEM_GRANT),
    )(*operands)


def ring_plan(d_blocks, d_index, row_perm, ks_blocks, ks_index, c_index):
    row_count = lax.axis_size("row")
    block_size = d_blocks.shape[-1]
    half_cols = row_perm.shape[0] // lax.axis_size("col")
    own = d_blocks.reshape(-1, block_size)
    slots = d_blocks.shape[2]
    lead = slots // 2
    tail = slots - lead
    label_rows = -(-slots // 8) * 8
    labels = jnp.pad(
        d_index[0, 0].astype(jnp.float32), ((0, label_rows - slots), (0, block_size - 2))
    )
    order = ring_order(row_count)
    forward = [(order[i], order[(i + 1) % row_count]) for i in range(row_count)]
    backward = [(b, a) for a, b in forward]
    twins = [(0, 1), (1, 0)]

    first_part = own[: lead * block_size]
    second_part = jnp.concatenate([own[lead * block_size :], labels], axis=0)
    pieces, chunks = [], []

    def arrived(first, second):
        pieces.append((lead, 0, len(pieces) + 1))
        pieces.append((tail, lead, None))
        chunks.extend([first, second])

    arrived(first_part, second_part)
    a_fwd = a_bwd = first_part
    b_fwd = b_bwd = second_part
    half = row_count // 2
    ks_own = ks_blocks.reshape(-1, block_size, block_size)
    for step in range(1, half):
        a_fwd = lax.ppermute(a_fwd, "row", forward)
        a_bwd = lax.ppermute(a_bwd, "row", backward)
        b_fwd = lax.ppermute(b_fwd, "row", forward)
        b_bwd = lax.ppermute(b_bwd, "row", backward)
        arrived(a_fwd, b_fwd)
        arrived(a_bwd, b_bwd)
        if step == 1:
            ks_twin = lax.ppermute(ks_own, "col", twins)
            ks_places = ks_index.reshape(ks_index.shape[1:])
            ks_places_twin = lax.ppermute(ks_places, "col", twins)
            parts, norms = split_ks(ks_own, ks_twin)
    a_fwd = lax.ppermute(a_fwd, "row", forward)
    b_bwd = lax.ppermute(b_bwd, "row", backward)

    tables = [row_perm, ks_places, ks_places_twin, c_index.reshape(-1)]
    stop_count = 2 * ks_blocks.shape[1]
    shape = (c_index.shape[-1], block_size, block_size)
    sizes = (row_count, stop_count, half_cols)
    partial = add_products(sizes, tables, parts, norms, None, pieces, chunks, shape)
    last = [(lead, 0, 1), (tail, lead, None)]
    total = add_products(sizes, tables, parts, norms, partial, last, [a_fwd, b_bwd], shape)
    return total.reshape(c_index.shape + (block_size, block_size))


def on_device(d_blocks, d_index, row_perm, ks_blocks, ks_index, c_index):
    rows, slots = lax.axis_size("row"), d_blocks.shape[2]
    gathered = rows * slots
    routed = rows * CAPX + 3 * (3 * rows // 2)
    plan = ring_plan if gathered <= routed else panel_plan
    return plan(d_blocks, d_index, row_perm, ks_blocks, ks_index, c_index)


def solution(mesh):
    return jax.shard_map(
        on_device,
        mesh=mesh,
        in_specs=(
            P(("groups", "row"), "col", None, None, None),
            P(("groups", "row"), "col", None, None),
            P("groups"),
            P(("groups", "row"), "col", None, None, None),
            P(("groups", "row"), "col", None),
            P(("groups", "row"), "col", None),
        ),
        out_specs=P(("groups", "row"), "col", None, None, None),
        check_vma=False,
    )
```

```python
import functools
import math

import jax
import jax.numpy as jnp
from jax import lax
from jax.experimental import pallas as pl
from jax.experimental.pallas import tpu as pltpu
from jax.sharding import PartitionSpec as P

BR = 4
CAPX = 2


FILTER = 0.055
UNROLL = 4
VMEM_GRANT = 8 * 1024 * 1024


def passed_along(shard, axis, by):
    size = lax.axis_size(axis)
    return lax.ppermute(shard, axis, [(i, (i + by) % size) for i in range(size)])


def window_blocks(slots, places):
    onehot = (places[:, None] == jnp.arange(BR * BR)[None, :]).astype(jnp.float32)
    return jnp.einsum("qp,qxy->pxy", onehot, slots, precision=lax.Precision.HIGHEST)


def block_norms(blocks):
    return jnp.sqrt(jnp.sum(blocks * blocks, axis=(-2, -1)))


def stop_product(density_panel, panel_labels, panel_norms, ks_slots, ks_places, targets, half_cols):
    block_size = density_panel.shape[-1]
    limit = FILTER * block_size * math.sqrt(block_size)
    window = window_blocks(ks_slots, ks_places)
    window_norms = block_norms(window)
    target_rows = targets // half_cols
    target_cols = targets % half_cols
    slot_range = jnp.arange(density_panel.shape[0])
    inner_rows = jnp.arange(BR)
    matches = (panel_labels[None, None, :, 0] == inner_rows[None, :, None]) & (
        panel_labels[None, None, :, 1] == target_cols[:, None, None]
    )
    present_pair = jnp.any(matches, axis=2)
    where_slot = jnp.sum(matches.astype(jnp.int32) * slot_range[None, None, :], axis=2)
    chosen = density_panel[where_slot]
    chosen_norms = panel_norms[where_slot]
    picked = target_rows[:, None] * BR + inner_rows[None, :]
    ks_norms = window_norms[picked]
    retained = present_pair & (ks_norms * chosen_norms >= limit)
    masked = jnp.where(retained[..., None, None], window[picked], 0.0)
    return jnp.einsum("tkxy,tkyz->txz", masked, chosen, precision=lax.Precision.HIGHEST)


def panel_plan(d_blocks, d_index, row_perm, ks_blocks, ks_index, c_index):
    row_count = lax.axis_size("row")
    block_size = d_blocks.shape[-1]
    blocks = d_blocks.reshape(-1, block_size, block_size)
    slot_list = d_index.reshape(-1, 2)
    block_rows = row_perm.shape[0]
    half_cols = block_rows // lax.axis_size("col")
    capacity = 3 * row_count // 2
    position = jnp.sum(
        jnp.where(slot_list[:, 0:1] == jnp.arange(block_rows)[None, :], row_perm[None, :], 0),
        axis=1,
    )
    grid_panel = position // BR
    inner_row = position % BR
    onehot = (grid_panel[:, None] == jnp.arange(row_count)[None, :]).astype(jnp.int32)
    arrival_rank = jnp.sum((jnp.cumsum(onehot, axis=0) - onehot) * onehot, axis=1)
    send_slot = grid_panel * CAPX + arrival_rank
    outgoing = (
        jnp.zeros((row_count * CAPX, block_size, block_size), jnp.float32).at[send_slot].set(blocks)
    )
    outgoing = outgoing.reshape(row_count, CAPX, block_size, block_size)
    labels = (
        jnp.full((row_count * CAPX, 2), -1, jnp.int32)
        .at[send_slot]
        .set(jnp.stack([inner_row, slot_list[:, 1]], axis=1))
    )
    labels = labels.reshape(row_count, CAPX, 2)
    arrived, arrived_labels = (
        lax.all_to_all(outgoing, "row", split_axis=0, concat_axis=0, tiled=True),
        lax.all_to_all(labels, "row", split_axis=0, concat_axis=0, tiled=True),
    )
    arrived = arrived.reshape(-1, block_size, block_size)
    arrived_labels = arrived_labels.reshape(-1, 2)
    keep_order = jnp.argsort((arrived_labels[:, 0] < 0).astype(jnp.int32), stable=True)[:capacity]
    density_panel = arrived[keep_order]
    panel_labels = arrived_labels[keep_order]
    ks_all, ks_places = (
        lax.all_gather(ks_blocks, "col", axis=1, tiled=True),
        lax.all_gather(ks_index, "col", axis=1, tiled=True),
    )
    ks_all = ks_all[0]
    ks_places = ks_places[0]
    targets = c_index.reshape(-1)
    stop_count = ks_all.shape[0]
    panel_norms = block_norms(density_panel)
    accumulated = jnp.zeros((targets.shape[0], block_size, block_size), jnp.float32)
    for station in range(stop_count):
        accumulated = accumulated + stop_product(
            density_panel,
            panel_labels,
            panel_norms,
            ks_all[station],
            ks_places[station],
            targets,
            half_cols,
        )
        if station + 1 < stop_count:
            density_panel, panel_labels, panel_norms = passed_along(
                (density_panel, panel_labels, panel_norms), "row", -1
            )
    return accumulated.reshape(c_index.shape + (block_size, block_size))


def ring_order(count):
    return list(range(0, count, 2)) + list(range(1, count, 2))[::-1]


def split_bf16(x):
    high = x.astype(jnp.bfloat16)
    return high, (x - high.astype(jnp.float32)).astype(jnp.bfloat16)


def norm_of(x):
    columns = jnp.sum(x * x, axis=0, keepdims=True)
    return jnp.sqrt(jnp.sum(columns, axis=1, keepdims=True))


def in_vmem(x):
    return pltpu.with_memory_space_constraint(x, pltpu.VMEM)


def in_hbm(x):
    return pltpu.with_memory_space_constraint(x, pltpu.HBM)


VMEM_SPEC = pl.BlockSpec(memory_space=pltpu.VMEM)
HBM_SPEC = pl.BlockSpec(memory_space=pltpu.HBM)
GRANT = pltpu.CompilerParams(vmem_limit_bytes=VMEM_GRANT)


def small_cost(microseconds):
    return pl.CostEstimate(flops=0, bytes_accessed=int(3.7e6 * microseconds), transcendentals=0)


def start_all(pairs, sems):
    copies = [pltpu.make_async_copy(src, dst, sems.at[n]) for n, (src, dst) in enumerate(pairs)]
    for copy in copies:
        copy.start()
    return copies


def pack_kernel(lead, index_ref, places_ref, blocks_ref, ks_ref, lead_ref, rest_ref, ks_out_ref, index, places, sems):
    slots = index.shape[3]
    width = lead_ref.shape[1]
    lead_rows = blocks_ref.shape[0] // slots * lead
    rest_rows = blocks_ref.shape[0] - lead_rows
    ks_rows = ks_ref.shape[0]
    copies = start_all(
        [
            (index_ref, index),
            (places_ref, places),
            (blocks_ref.at[pl.ds(0, lead_rows)], lead_ref.at[pl.ds(0, lead_rows)]),
            (blocks_ref.at[pl.ds(lead_rows, rest_rows)], rest_ref.at[pl.ds(0, rest_rows)]),
            (ks_ref, ks_out_ref.at[pl.ds(0, ks_rows)]),
        ],
        sems,
    )

    def label_rows(ref, rows, numbers):
        shape = (ref.shape[0] - rows, width)
        line = lax.broadcasted_iota(jnp.int32, shape, 0)
        lane = lax.broadcasted_iota(jnp.int32, shape, 1)
        labels = jnp.zeros(shape, jnp.int32)
        for (x, y), number in numbers:
            labels = jnp.where((line == x) & (lane == y), number, labels)
        ref[pl.ds(rows, shape[0]), :] = labels.astype(jnp.float32)

    copies[0].wait()
    copies[1].wait()
    for ref, rows, first, count in ((lead_ref, lead_rows, 0, lead), (rest_ref, rest_rows, lead, slots - lead)):
        label_rows(
            ref,
            rows,
            [((n, field), index[0, 0, field, first + n]) for n in range(count) for field in range(2)],
        )
    _, stops, present = places.shape
    label_rows(
        ks_out_ref, ks_rows, [((x, y), places[0, x, y]) for x in range(stops) for y in range(present)]
    )
    for copy in copies[2:]:
        copy.wait()


def pack(blocks, index, ks, places, lead):
    slots = index.shape[3]
    rows, width = blocks.shape
    ks_rows = ks.shape[0]
    lead_rows = rows // slots * lead
    return pl.pallas_call(
        functools.partial(pack_kernel, lead),
        out_shape=(
            pltpu.VMEM((lead_rows + -(-lead // 8) * 8, width), jnp.float32),
            pltpu.VMEM((rows - lead_rows + -(-(slots - lead) // 8) * 8, width), jnp.float32),
            pltpu.VMEM((ks_rows + -(-places.shape[1] // 8) * 8, width), jnp.float32),
        ),
        in_specs=[HBM_SPEC] * 4,
        out_specs=(VMEM_SPEC,) * 3,
        scratch_shapes=[
            pltpu.SMEM(index.shape, jnp.int32),
            pltpu.SMEM(places.shape, jnp.int32),
            pltpu.SemaphoreType.DMA((5,)),
        ],
        compiler_params=GRANT,
        cost_estimate=small_cost(1),
    )(*map(in_hbm, (index, places, blocks, ks)))


def window_kernel(
    half_cols, present, perm_ref, target_ref, own_ref, twin_ref, parts_ref, norms_ref, table_ref,
    perm, targets, own_place, twin_place, table, sems, out_sem,
):
    block_size = own_ref.shape[1]
    count = parts_ref.shape[0] // 2
    half_stops = count // present
    ks_rows = count * block_size
    col = lax.axis_index("col")
    ks_cells = 2 * half_stops * BR * BR
    target_cells = BR * half_cols
    place_rows = pl.ds(ks_rows, own_ref.shape[0] - ks_rows)
    copies = start_all(
        [
            (perm_ref, perm),
            (target_ref, targets),
            (own_ref.at[place_rows], own_place),
            (twin_ref.at[place_rows], twin_place),
        ],
        sems,
    )
    for i in range(ks_cells + target_cells):
        table[i] = -1
    for copy in copies:
        copy.wait()
    for i in range(perm.shape[0]):
        table[ks_cells + target_cells + i] = perm[i]
    for t in range(targets.shape[2]):
        table[ks_cells + targets[0, 0, t]] = t
    for local in range(half_stops):
        own_base = (col * half_stops + local) * BR * BR
        twin_base = ((1 - col) * half_stops + local) * BR * BR
        for q in range(present):
            table[own_base + own_place[local, q].astype(jnp.int32)] = local * present + q
            table[twin_base + twin_place[local, q].astype(jnp.int32)] = (half_stops + local) * present + q
    publish = pltpu.make_async_copy(table, table_ref, out_sem)
    publish.start()
    for half, ref in enumerate((own_ref, twin_ref)):

        def one(q, _, half=half, ref=ref):
            block = ref[pl.ds(pl.multiple_of(q * block_size, block_size), block_size), :]
            parts_ref[half * count + q] = jnp.concatenate(split_bf16(block), axis=1)
            norms_ref[half * count + q] = jnp.broadcast_to(norm_of(block), norms_ref.shape[1:])

        lax.fori_loop(0, count, one, None, unroll=4)
    publish.wait()


def prepare_window(row_perm, targets, own, twin, half_cols, half_stops, present):
    rows, block_size = own.shape
    count = half_stops * present
    place_rows = rows - count * block_size
    cells = 2 * half_stops * BR * BR + BR * half_cols + row_perm.shape[0]
    cells = -(-cells // 128) * 128
    return pl.pallas_call(
        functools.partial(window_kernel, half_cols, present),
        out_shape=(
            pltpu.VMEM((2 * count, block_size, 2 * block_size), jnp.bfloat16),
            pltpu.VMEM((2 * count, 1, block_size), jnp.float32),
            pltpu.VMEM((cells,), jnp.int32),
        ),
        in_specs=[HBM_SPEC] * 2 + [VMEM_SPEC] * 2,
        out_specs=(VMEM_SPEC,) * 3,
        scratch_shapes=[
            pltpu.SMEM(row_perm.shape, jnp.int32),
            pltpu.SMEM(targets.shape, jnp.int32),
            pltpu.SMEM((place_rows, block_size), jnp.float32),
            pltpu.SMEM((place_rows, block_size), jnp.float32),
            pltpu.SMEM((cells,), jnp.int32),
            pltpu.SemaphoreType.DMA((4,)),
            pltpu.SemaphoreType.DMA,
        ],
        compiler_params=GRANT,
        cost_estimate=small_cost(2),
    )(in_hbm(row_perm), in_hbm(targets), in_vmem(own), in_vmem(twin))


def product_kernel(config, *refs):
    row_count, stop_count, half_cols, limit, pieces, first, final = config
    table_ref, parts_ref, norms_ref = refs[:3]
    chunk_refs = refs[3 : 3 + len(pieces)]
    rest = refs[3 + len(pieces) + (not first) + (final == "touched") :]
    c_ref = rest[0]
    if final:
        out_ref = rest[1]
        rest = rest[1:]
    table, label, list_t, list_q, list_b, touched, held, sems, out_sems = rest[1:]
    block_size = c_ref.shape[-1]
    row = lax.axis_index("row")
    ks_cells = stop_count * BR * BR
    perm_at = ks_cells + BR * half_cols

    moves = [(table_ref, table)]
    for number, blocks in enumerate(pieces):
        rows = pl.ds(blocks * block_size, label.shape[1])
        moves.append((chunk_refs[number].at[rows], label.at[number]))
    copies = start_all(moves, sems)
    if first:
        c_ref[...] = jnp.zeros_like(c_ref)
    for copy in copies:
        copy.wait()

    found = (jnp.int32(0), jnp.int32(0))
    for number, blocks in enumerate(pieces):

        def look(b, found, number=number, chunk_ref=chunk_refs[number]):
            pairs, kept = found
            position = table[perm_at + label[number, b, 0].astype(jnp.int32)]
            column = label[number, b, 1].astype(jnp.int32)
            behind = lax.div(position, BR) - row
            stop = jnp.where(behind < 0, behind + row_count, behind)
            in_window = stop < stop_count
            place = jnp.minimum(stop, stop_count - 1) * BR * BR + lax.rem(position, BR)
            before = pairs
            for i in range(BR):
                target = table[ks_cells + i * half_cols + column]
                ks = table[place + i * BR]
                list_t[pairs] = target
                list_q[pairs] = ks
                list_b[pairs] = kept
                hit = (target >= 0) & (ks >= 0) & in_window
                pairs = pairs + hit.astype(jnp.int32)
            some = pairs > before

            @pl.when(some)
            def _():
                held[kept] = chunk_ref[pl.ds(pl.multiple_of(b * block_size, block_size), block_size), :]

            return pairs, kept + some.astype(jnp.int32)

        found = lax.fori_loop(0, blocks, look, found)
    pairs, _ = found
    for u in range(UNROLL):
        list_t[pairs + u] = 0
        list_q[pairs + u] = 0
        list_b[pairs + u] = 0

    def multiply(step, _):
        for u in range(UNROLL):
            at = step * UNROLL + u
            target, ks, slot = list_t[at], list_q[at], list_b[at]
            density = held[slot]
            bound = jnp.where(at < pairs, limit, jnp.inf)
            keep = norms_ref[ks] * norm_of(density) >= bound
            high, low = split_bf16(density)
            weights = jnp.concatenate(
                [
                    jnp.concatenate([high, low], axis=1),
                    jnp.concatenate([high, jnp.zeros_like(low)], axis=1),
                ],
                axis=0,
            )
            both = jnp.dot(parts_ref[ks], weights, preferred_element_type=jnp.float32)
            value = both[:, :block_size] + both[:, block_size:]
            c_ref[target] += jnp.where(keep, value, 0.0)

    lax.fori_loop(0, lax.div(pairs + UNROLL - 1, UNROLL), multiply, None)
    if final == "whole":
        copy = pltpu.make_async_copy(c_ref, out_ref, out_sems.at[0])
        copy.start()
        copy.wait()
    elif final == "touched":
        targets = c_ref.shape[0]
        for t in range(targets):
            touched[t] = 0

        def touch(p, _):
            touched[list_t[p]] = 1

        lax.fori_loop(0, pairs, touch, None)
        for begin in (True, False):
            for t in range(targets):
                copy = pltpu.make_async_copy(c_ref.at[t], out_ref.at[t], out_sems.at[t])

                @pl.when(touched[t] == 1)
                def _(copy=copy, begin=begin):
                    (copy.start if begin else copy.wait)()


def add_products(sizes, window, accumulated, pieces, chunks, shape, final=None, written=None):
    block_size = shape[-1]
    limit = FILTER * block_size * math.sqrt(block_size)
    first = accumulated is None
    blocks = sum(pieces)
    label_rows = -(-max(pieces) // 8) * 8
    parts, norms, table = window
    operands = [*map(in_vmem, (table, parts, norms, *chunks))]
    aliases = {}
    if not first:
        aliases = {len(operands): 0}
        operands.append(in_vmem(accumulated))
    if written is not None:
        aliases[len(operands)] = 1
        operands.append(in_hbm(written))
    in_specs = [VMEM_SPEC] * (len(operands) - (written is not None)) + [HBM_SPEC] * (written is not None)
    longest = blocks * BR + 2 * UNROLL
    outs = 1 if final is None else 2
    out_shape = [pltpu.VMEM(shape, jnp.float32), pltpu.HBM(shape, jnp.float32)][:outs]
    return pl.pallas_call(
        functools.partial(product_kernel, (*sizes, limit, pieces, first, final)),
        out_shape=out_shape,
        in_specs=in_specs,
        out_specs=[VMEM_SPEC, HBM_SPEC][:outs],
        scratch_shapes=[
            pltpu.SMEM(table.shape, jnp.int32),
            pltpu.SMEM((len(pieces), label_rows, block_size), jnp.float32),
            pltpu.SMEM((longest,), jnp.int32),
            pltpu.SMEM((longest,), jnp.int32),
            pltpu.SMEM((longest,), jnp.int32),
            pltpu.SMEM((shape[0],), jnp.int32),
            pltpu.VMEM((blocks, block_size, block_size), jnp.float32),
            pltpu.SemaphoreType.DMA((1 + len(pieces),)),
            pltpu.SemaphoreType.DMA((shape[0],)),
        ],
        input_output_aliases=aliases,
        compiler_params=GRANT,
        cost_estimate=small_cost(2),
    )(*operands)


def tied(values, token):
    return lax.optimization_barrier((*values, token))[:-1]


def ring_plan(d_blocks, d_index, row_perm, ks_blocks, ks_index, c_index):
    row_count = lax.axis_size("row")
    block_size = d_blocks.shape[-1]
    half_cols = row_perm.shape[0] // lax.axis_size("col")
    slots = d_blocks.shape[2]
    lead = slots // 2
    order = ring_order(row_count)
    forward = [(order[i], order[(i + 1) % row_count]) for i in range(row_count)]
    backward = [(b, a) for a, b in forward]
    twins = [(0, 1), (1, 0)]
    stop_count = 2 * ks_blocks.shape[1]
    shape = (c_index.shape[-1], block_size, block_size)
    sizes = (row_count, stop_count, half_cols)

    _, half_stops, present = ks_index.shape
    a_fwd, b_fwd, ks_own = pack(
        d_blocks.reshape(-1, block_size),
        jnp.swapaxes(d_index, 2, 3),
        ks_blocks.reshape(-1, block_size),
        ks_index,
        lead,
    )
    a_bwd, b_bwd = a_fwd, b_fwd
    ks_twin = lax.ppermute(ks_own, "col", twins)
    window = prepare_window(row_perm, c_index, ks_own, ks_twin, half_cols, half_stops, present)
    pieces, chunks = [], []
    accumulated = None

    def arrived(first, second):
        pieces.extend([lead, slots - lead])
        chunks.extend([first, second])

    arrived(a_fwd, b_fwd)
    written = []
    half = row_count // 2
    for step in range(1, half + 1):
        a_fwd = lax.ppermute(a_fwd, "row", forward)
        b_bwd = lax.ppermute(b_bwd, "row", backward)
        if step > 1:
            if step > 2:
                (accumulated,) = tied((accumulated,), ready)
            final = {half - 1: "whole", half: "touched"}.get(step)
            accumulated, *written = add_products(
                sizes, window, accumulated, pieces, chunks, shape, final, *written
            )
            pieces, chunks = [], []
        if step < half:
            if step > 1:
                a_bwd, b_fwd = tied((a_bwd, b_fwd), window[1] if step == 2 else before)
            before = accumulated
            a_bwd = lax.ppermute(a_bwd, "row", backward)
            b_fwd = lax.ppermute(b_fwd, "row", forward)
            arrived(a_fwd, b_fwd)
            arrived(a_bwd, b_bwd)
            ready = a_fwd
    arrived(a_fwd, b_bwd)
    _, total = add_products(
        sizes, window, accumulated, pieces, chunks, shape, "touched", written[0]
    )
    return total.reshape(c_index.shape + (block_size, block_size))


def on_device(d_blocks, d_index, row_perm, ks_blocks, ks_index, c_index):
    rows, slots = lax.axis_size("row"), d_blocks.shape[2]
    gathered = rows * slots
    routed = rows * CAPX + 3 * (3 * rows // 2)
    plan = ring_plan if gathered <= routed else panel_plan
    return plan(d_blocks, d_index, row_perm, ks_blocks, ks_index, c_index)


def solution(mesh):
    return jax.shard_map(
        on_device,
        mesh=mesh,
        in_specs=(
            P(("groups", "row"), "col", None, None, None),
            P(("groups", "row"), "col", None, None),
            P("groups"),
            P(("groups", "row"), "col", None, None, None),
            P(("groups", "row"), "col", None),
            P(("groups", "row"), "col", None),
        ),
        out_specs=P(("groups", "row"), "col", None, None, None),
        check_vma=False,
    )
```

```python
import functools
import math

import jax
import jax.numpy as jnp
from jax import lax
from jax.experimental import pallas as pl
from jax.experimental.pallas import tpu as pltpu
from jax.sharding import PartitionSpec as P

BR = 4
CAPX = 2


FILTER = 0.055
UNROLL = 4
VMEM_GRANT = 8 * 1024 * 1024


def passed_along(shard, axis, by):
    size = lax.axis_size(axis)
    return lax.ppermute(shard, axis, [(i, (i + by) % size) for i in range(size)])


def window_blocks(slots, places):
    onehot = (places[:, None] == jnp.arange(BR * BR)[None, :]).astype(jnp.float32)
    return jnp.einsum("qp,qxy->pxy", onehot, slots, precision=lax.Precision.HIGHEST)


def block_norms(blocks):
    return jnp.sqrt(jnp.sum(blocks * blocks, axis=(-2, -1)))


def stop_product(density_panel, panel_labels, panel_norms, ks_slots, ks_places, targets, half_cols):
    block_size = density_panel.shape[-1]
    limit = FILTER * block_size * math.sqrt(block_size)
    window = window_blocks(ks_slots, ks_places)
    window_norms = block_norms(window)
    target_rows = targets // half_cols
    target_cols = targets % half_cols
    slot_range = jnp.arange(density_panel.shape[0])
    inner_rows = jnp.arange(BR)
    matches = (panel_labels[None, None, :, 0] == inner_rows[None, :, None]) & (
        panel_labels[None, None, :, 1] == target_cols[:, None, None]
    )
    present_pair = jnp.any(matches, axis=2)
    where_slot = jnp.sum(matches.astype(jnp.int32) * slot_range[None, None, :], axis=2)
    chosen = density_panel[where_slot]
    chosen_norms = panel_norms[where_slot]
    picked = target_rows[:, None] * BR + inner_rows[None, :]
    ks_norms = window_norms[picked]
    retained = present_pair & (ks_norms * chosen_norms >= limit)
    masked = jnp.where(retained[..., None, None], window[picked], 0.0)
    return jnp.einsum("tkxy,tkyz->txz", masked, chosen, precision=lax.Precision.HIGHEST)


def panel_plan(d_blocks, d_index, row_perm, ks_blocks, ks_index, c_index):
    row_count = lax.axis_size("row")
    block_size = d_blocks.shape[-1]
    blocks = d_blocks.reshape(-1, block_size, block_size)
    slot_list = d_index.reshape(-1, 2)
    block_rows = row_perm.shape[0]
    half_cols = block_rows // lax.axis_size("col")
    capacity = 3 * row_count // 2
    position = jnp.sum(
        jnp.where(slot_list[:, 0:1] == jnp.arange(block_rows)[None, :], row_perm[None, :], 0),
        axis=1,
    )
    grid_panel = position // BR
    inner_row = position % BR
    onehot = (grid_panel[:, None] == jnp.arange(row_count)[None, :]).astype(jnp.int32)
    arrival_rank = jnp.sum((jnp.cumsum(onehot, axis=0) - onehot) * onehot, axis=1)
    send_slot = grid_panel * CAPX + arrival_rank
    outgoing = (
        jnp.zeros((row_count * CAPX, block_size, block_size), jnp.float32).at[send_slot].set(blocks)
    )
    outgoing = outgoing.reshape(row_count, CAPX, block_size, block_size)
    labels = (
        jnp.full((row_count * CAPX, 2), -1, jnp.int32)
        .at[send_slot]
        .set(jnp.stack([inner_row, slot_list[:, 1]], axis=1))
    )
    labels = labels.reshape(row_count, CAPX, 2)
    arrived, arrived_labels = (
        lax.all_to_all(outgoing, "row", split_axis=0, concat_axis=0, tiled=True),
        lax.all_to_all(labels, "row", split_axis=0, concat_axis=0, tiled=True),
    )
    arrived = arrived.reshape(-1, block_size, block_size)
    arrived_labels = arrived_labels.reshape(-1, 2)
    keep_order = jnp.argsort((arrived_labels[:, 0] < 0).astype(jnp.int32), stable=True)[:capacity]
    density_panel = arrived[keep_order]
    panel_labels = arrived_labels[keep_order]
    ks_all, ks_places = (
        lax.all_gather(ks_blocks, "col", axis=1, tiled=True),
        lax.all_gather(ks_index, "col", axis=1, tiled=True),
    )
    ks_all = ks_all[0]
    ks_places = ks_places[0]
    targets = c_index.reshape(-1)
    stop_count = ks_all.shape[0]
    panel_norms = block_norms(density_panel)
    accumulated = jnp.zeros((targets.shape[0], block_size, block_size), jnp.float32)
    for station in range(stop_count):
        accumulated = accumulated + stop_product(
            density_panel,
            panel_labels,
            panel_norms,
            ks_all[station],
            ks_places[station],
            targets,
            half_cols,
        )
        if station + 1 < stop_count:
            density_panel, panel_labels, panel_norms = passed_along(
                (density_panel, panel_labels, panel_norms), "row", -1
            )
    return accumulated.reshape(c_index.shape + (block_size, block_size))


def ring_order(count):
    return list(range(0, count, 2)) + list(range(1, count, 2))[::-1]


def split_bf16(x):
    high = x.astype(jnp.bfloat16)
    return high, (x - high.astype(jnp.float32)).astype(jnp.bfloat16)


def norm_of(x):
    columns = jnp.sum(x * x, axis=0, keepdims=True)
    return jnp.sqrt(jnp.sum(columns, axis=1, keepdims=True))


def in_vmem(x):
    return pltpu.with_memory_space_constraint(x, pltpu.VMEM)


def in_hbm(x):
    return pltpu.with_memory_space_constraint(x, pltpu.HBM)


VMEM_SPEC = pl.BlockSpec(memory_space=pltpu.VMEM)
HBM_SPEC = pl.BlockSpec(memory_space=pltpu.HBM)
GRANT = pltpu.CompilerParams(vmem_limit_bytes=VMEM_GRANT)


def small_cost(microseconds):
    return pl.CostEstimate(flops=0, bytes_accessed=int(3.7e6 * microseconds), transcendentals=0)


def start_all(pairs, sems):
    copies = [pltpu.make_async_copy(src, dst, sems.at[n]) for n, (src, dst) in enumerate(pairs)]
    for copy in copies:
        copy.start()
    return copies


def write_labels(ref, rows, numbers):
    shape = (ref.shape[0] - rows, ref.shape[1])
    line = lax.broadcasted_iota(jnp.int32, shape, 0)
    lane = lax.broadcasted_iota(jnp.int32, shape, 1)
    labels = jnp.zeros(shape, jnp.int32)
    for (x, y), number in numbers:
        labels = jnp.where((line == x) & (lane == y), number, labels)
    ref[pl.ds(rows, shape[0]), :] = labels.astype(jnp.float32)


def pack_kernel(lead, index_ref, blocks_ref, lead_ref, rest_ref, index, sems):
    slots = index.shape[3]
    lead_rows = blocks_ref.shape[0] // slots * lead
    rest_rows = blocks_ref.shape[0] - lead_rows
    copies = start_all(
        [
            (index_ref, index),
            (blocks_ref.at[pl.ds(0, lead_rows)], lead_ref.at[pl.ds(0, lead_rows)]),
            (blocks_ref.at[pl.ds(lead_rows, rest_rows)], rest_ref.at[pl.ds(0, rest_rows)]),
        ],
        sems,
    )
    copies[0].wait()
    for ref, rows, first, count in ((lead_ref, lead_rows, 0, lead), (rest_ref, rest_rows, lead, slots - lead)):
        write_labels(
            ref,
            rows,
            [((n, field), index[0, 0, field, first + n]) for n in range(count) for field in range(2)],
        )
    for copy in copies[1:]:
        copy.wait()


def pack(blocks, index, lead):
    slots = index.shape[3]
    rows, width = blocks.shape
    lead_rows = rows // slots * lead
    return pl.pallas_call(
        functools.partial(pack_kernel, lead),
        out_shape=(
            pltpu.VMEM((lead_rows + -(-lead // 8) * 8, width), jnp.float32),
            pltpu.VMEM((rows - lead_rows + -(-(slots - lead) // 8) * 8, width), jnp.float32),
        ),
        in_specs=[HBM_SPEC] * 2,
        out_specs=(VMEM_SPEC,) * 2,
        scratch_shapes=[pltpu.SMEM(index.shape, jnp.int32), pltpu.SemaphoreType.DMA((3,))],
        compiler_params=GRANT,
        cost_estimate=small_cost(1),
    )(in_hbm(index), in_hbm(blocks))


def lines_of(entries, lanes):
    return -(-entries * BR // lanes)


def window_kernel(half_cols, *refs):
    hbm_refs, twin_ref = refs[:5], refs[5]
    parts_ref, norms_ref, table_ref = refs[6:9]
    perm, own_place, twin_place, targets, own = refs[9:14]
    stop_at, table, sems, out_sem = refs[14:]
    lanes = table.shape[1]
    column_line = lines_of(perm.shape[0], lanes)
    row, row_count = lax.axis_index("row"), lax.axis_size("row")
    count = own.shape[0]
    _, half_stops, present = own_place.shape
    col = lax.axis_index("col")
    copies = start_all(list(zip(hbm_refs, refs[9:14])), sems)

    def split_half(half, ref):
        def one(q, _):
            block = ref[q]
            parts_ref[half * count + q] = jnp.concatenate(split_bf16(block), axis=1)
            norms_ref[half * count + q] = jnp.broadcast_to(norm_of(block), norms_ref.shape[1:])

        lax.fori_loop(0, count, one, None, unroll=4)

    split_half(1, twin_ref)
    for i in range(stop_at.shape[0]):
        stop_at[i] = -1
    for cell in range(half_cols * BR):
        table[column_line + cell // lanes, cell % lanes] = -1.0
    for copy in copies[:4]:
        copy.wait()
    for local in range(half_stops):
        own_base = (col * half_stops + local) * BR * BR
        twin_base = ((1 - col) * half_stops + local) * BR * BR
        for q in range(present):
            stop_at[own_base + own_place[0, local, q]] = local * present + q
            stop_at[twin_base + twin_place[0, local, q]] = (half_stops + local) * present + q
    for t in range(targets.shape[2]):
        place = targets[0, 0, t]
        cell = lax.rem(place, half_cols) * BR + lax.div(place, half_cols)
        table[column_line + lax.div(cell, lanes), lax.rem(cell, lanes)] = jnp.float32(t)
    for block_row in range(perm.shape[0]):
        behind = lax.div(perm[block_row], BR) - row
        stop = jnp.where(behind < 0, behind + row_count, behind)
        place = jnp.minimum(stop, 2 * half_stops - 1) * BR * BR + lax.rem(perm[block_row], BR)
        for i in range(BR):
            cell = block_row * BR + i
            slot = jnp.where(stop < 2 * half_stops, stop_at[place + i * BR], -1)
            table[cell // lanes, cell % lanes] = slot.astype(jnp.float32)
    publish = pltpu.make_async_copy(table, table_ref, out_sem)
    publish.start()
    copies[4].wait()
    split_half(0, own)
    publish.wait()


def prepare_window(row_perm, own_places, twin_places, targets, own, twin, half_cols):
    count, block_size, _ = own.shape
    lines = lines_of(row_perm.shape[0], block_size) + lines_of(half_cols, block_size)
    lines = -(-lines // 8) * 8
    held = [row_perm, own_places, twin_places, targets]
    return pl.pallas_call(
        functools.partial(window_kernel, half_cols),
        out_shape=(
            pltpu.VMEM((2 * count, block_size, 2 * block_size), jnp.bfloat16),
            pltpu.VMEM((2 * count, 1, block_size), jnp.float32),
            pltpu.VMEM((lines, block_size), jnp.float32),
        ),
        in_specs=[HBM_SPEC] * 5 + [VMEM_SPEC],
        out_specs=(VMEM_SPEC,) * 3,
        scratch_shapes=[
            *(pltpu.SMEM(x.shape, jnp.int32) for x in held),
            pltpu.VMEM(own.shape, jnp.float32),
            pltpu.SMEM((2 * own_places.shape[1] * BR * BR,), jnp.int32),
            pltpu.SMEM((lines, block_size), jnp.float32),
            pltpu.SemaphoreType.DMA((5,)),
            pltpu.SemaphoreType.DMA,
        ],
        compiler_params=GRANT,
        cost_estimate=small_cost(2),
    )(*map(in_hbm, held), in_hbm(own), in_vmem(twin))


def product_kernel(config, *refs):
    block_rows, half_cols, limit, pieces, first, final = config
    table_ref, parts_ref, norms_ref = refs[:3]
    chunk_refs = refs[3 : 3 + len(pieces)]
    rest = refs[3 + len(pieces) + (not first) + (final == "touched") :]
    c_ref = rest[0]
    if final:
        out_ref = rest[1]
        rest = rest[1:]
    listed, touched, held, out_sems = rest[1:]
    block_size = c_ref.shape[-1]
    slot_bits = (parts_ref.shape[0] - 1).bit_length()
    code_bits = slot_bits + c_ref.shape[0].bit_length()
    slot_mask, none = (1 << slot_bits) - 1, (1 << code_bits) - 1
    per_word = 2 if 2 * code_bits < 32 else 1

    def target_of(entry):
        return (entry & none) >> slot_bits

    if first:
        c_ref[...] = jnp.zeros_like(c_ref)

    lane = lax.broadcasted_iota(jnp.int32, (1, block_size), 1).astype(jnp.float32)
    slot_lines = lines_of(block_rows, block_size)
    target_lines = lines_of(half_cols, block_size)

    def look_up(cells, first_line, lines):
        found = 0.0
        for n in range(lines):
            line = table_ref[pl.ds(first_line + n, 1), :]
            hit = cells - float(n * block_size) == lane
            found += jnp.sum(jnp.where(hit, line, 0.0), axis=1, keepdims=True)
        return found

    pairs, kept = jnp.int32(0), jnp.int32(0)
    words = []
    for chunk_ref, blocks in zip(chunk_refs, pieces):
        labels = chunk_ref[pl.ds(blocks * block_size, chunk_ref.shape[0] - blocks * block_size), :]
        for i in range(BR):
            slot = look_up(labels[:, 0:1] * float(BR) + float(i), 0, slot_lines)
            target = look_up(labels[:, 1:2] * float(BR) + float(i), slot_lines, target_lines)
            present = (slot >= 0.0) & (target >= 0.0)
            code = jnp.where(present, target * float(1 << slot_bits) + slot, float(none)).astype(jnp.int32)
            if i % per_word:
                words[-1] = words[-1] + (code << (code_bits * (i % per_word)))
            else:
                words.append(code)
    read = [
        [words[number * (BR // per_word) + w][b, 0] for w in range(BR // per_word)]
        for number, blocks in enumerate(pieces)
        for b in range(blocks)
    ]
    for number, (chunk_ref, blocks) in enumerate(zip(chunk_refs, pieces)):
        for b in range(blocks):
            before = pairs
            for word in read.pop(0):
                for n in range(per_word):
                    code = (word >> (code_bits * n)) & none
                    listed[pairs] = code + (kept << code_bits)
                    pairs = pairs + (code != none).astype(jnp.int32)
            held[kept] = chunk_ref[pl.ds(b * block_size, block_size), :]
            kept = kept + (pairs > before).astype(jnp.int32)
    for u in range(UNROLL):
        listed[pairs + u] = 0

    def multiply(step, _):
        for u in range(UNROLL):
            at = step * UNROLL + u
            entry = listed[at]
            ks, target, slot = entry & slot_mask, target_of(entry), entry >> code_bits
            density = held[slot]
            bound = jnp.where(at < pairs, limit, jnp.inf)
            keep = norms_ref[ks] * norm_of(density) >= bound
            high, low = split_bf16(density)
            weights = jnp.concatenate(
                [
                    jnp.concatenate([high, low], axis=1),
                    jnp.concatenate([high, jnp.zeros_like(low)], axis=1),
                ],
                axis=0,
            )
            both = jnp.dot(parts_ref[ks], weights, preferred_element_type=jnp.float32)
            value = both[:, :block_size] + both[:, block_size:]
            c_ref[target] += jnp.where(keep, value, 0.0)

    lax.fori_loop(0, lax.div(pairs + UNROLL - 1, UNROLL), multiply, None)
    if final == "whole":
        copy = pltpu.make_async_copy(c_ref, out_ref, out_sems.at[0])
        copy.start()
        copy.wait()
    elif final == "touched":
        targets = c_ref.shape[0]
        for t in range(targets):
            touched[t] = 0

        def touch(p, _):
            touched[target_of(listed[p])] = 1

        lax.fori_loop(0, pairs, touch, None)
        for begin in (True, False):
            for t in range(targets):
                copy = pltpu.make_async_copy(c_ref.at[t], out_ref.at[t], out_sems.at[t])

                @pl.when(touched[t] == 1)
                def _(copy=copy, begin=begin):
                    (copy.start if begin else copy.wait)()


def add_products(sizes, window, accumulated, group, shape, final=None, written=None):
    block_size = shape[-1]
    limit = FILTER * block_size * math.sqrt(block_size)
    first = accumulated is None
    pieces = [count for count, _ in group]
    chunks = [chunk for _, chunk in group]
    blocks = sum(pieces)
    parts, norms, table = window
    operands = [*map(in_vmem, (table, parts, norms, *chunks))]
    aliases = {}
    if not first:
        aliases = {len(operands): 0}
        operands.append(in_vmem(accumulated))
    if written is not None:
        aliases[len(operands)] = 1
        operands.append(in_hbm(written))
    in_specs = [VMEM_SPEC] * (len(operands) - (written is not None)) + [HBM_SPEC] * (written is not None)
    longest = blocks * BR + 2 * UNROLL
    outs = 1 if final is None else 2
    out_shape = [pltpu.VMEM(shape, jnp.float32), pltpu.HBM(shape, jnp.float32)][:outs]
    return pl.pallas_call(
        functools.partial(product_kernel, (*sizes, limit, pieces, first, final)),
        out_shape=out_shape,
        in_specs=in_specs,
        out_specs=[VMEM_SPEC, HBM_SPEC][:outs],
        scratch_shapes=[
            pltpu.SMEM((longest,), jnp.int32),
            pltpu.SMEM((shape[0],), jnp.int32),
            pltpu.VMEM((blocks, block_size, block_size), jnp.float32),
            pltpu.SemaphoreType.DMA((shape[0],)),
        ],
        input_output_aliases=aliases,
        compiler_params=GRANT,
        cost_estimate=small_cost(2),
    )(*operands)


def tied(values, token):
    return lax.optimization_barrier((*values, token))[:-1]


def ring_plan(d_blocks, d_index, row_perm, ks_blocks, ks_index, c_index):
    row_count = lax.axis_size("row")
    block_size = d_blocks.shape[-1]
    half_cols = row_perm.shape[0] // lax.axis_size("col")
    slots = d_blocks.shape[2]
    lead = slots // 2
    order = ring_order(row_count)
    forward = [(order[i], order[(i + 1) % row_count]) for i in range(row_count)]
    backward = [(b, a) for a, b in forward]
    twins = [(0, 1), (1, 0)]
    shape = (c_index.shape[-1], block_size, block_size)
    sizes = (row_perm.shape[0], half_cols)

    a_fwd, b_fwd = pack(d_blocks.reshape(-1, block_size), jnp.swapaxes(d_index, 2, 3), lead)
    a_bwd, b_bwd = a_fwd, b_fwd
    ks_own = ks_blocks.reshape(-1, block_size, block_size)
    ks_twin = lax.ppermute(ks_own, "col", twins)
    places_twin = lax.ppermute(ks_index, "col", twins)
    window = prepare_window(row_perm, ks_index, places_twin, c_index, ks_own, ks_twin, half_cols)
    accumulated, written = None, []
    group = [(lead, a_fwd), (slots - lead, b_bwd)]
    half = row_count // 2
    for step in range(1, half + 1):
        a_fwd = lax.ppermute(a_fwd, "row", forward)
        b_bwd = lax.ppermute(b_bwd, "row", backward)
        if step > 1:
            final = {half - 1: "whole", half: "touched"}.get(step)
            if step == half - 1:
                (accumulated,) = tied((accumulated,), a_fwd)
                group += [(lead, a_fwd), (slots - lead, b_bwd)]
            accumulated, *written = add_products(sizes, window, accumulated, group, shape, final, *written)
            group = []
        if step < half:
            if step > 1:
                token = window[1] if step == 2 else before
                (a_bwd,) = tied((a_bwd,), token)
                (b_fwd,) = tied((b_fwd,), token)
            before = accumulated
            a_bwd = lax.ppermute(a_bwd, "row", backward)
            b_fwd = lax.ppermute(b_fwd, "row", forward)
            if step < half - 1:
                group += [(lead, a_fwd), (slots - lead, b_bwd)]
            group += [(lead, a_bwd), (slots - lead, b_fwd)]
    group = [(lead, a_fwd), (slots - lead, b_bwd)]
    _, total = add_products(sizes, window, accumulated, group, shape, "touched", *written)
    return total.reshape(c_index.shape + (block_size, block_size))


def on_device(d_blocks, d_index, row_perm, ks_blocks, ks_index, c_index):
    rows, slots = lax.axis_size("row"), d_blocks.shape[2]
    gathered = rows * slots
    routed = rows * CAPX + 3 * (3 * rows // 2)
    plan = ring_plan if gathered <= routed else panel_plan
    return plan(d_blocks, d_index, row_perm, ks_blocks, ks_index, c_index)


def solution(mesh):
    return jax.shard_map(
        on_device,
        mesh=mesh,
        in_specs=(
            P(("groups", "row"), "col", None, None, None),
            P(("groups", "row"), "col", None, None),
            P("groups"),
            P(("groups", "row"), "col", None, None, None),
            P(("groups", "row"), "col", None),
            P(("groups", "row"), "col", None),
        ),
        out_specs=P(("groups", "row"), "col", None, None, None),
        check_vma=False,
    )
```

```python
import functools
import math

import jax
import jax.numpy as jnp
from jax import lax
from jax.experimental import pallas as pl
from jax.experimental.pallas import tpu as pltpu
from jax.sharding import PartitionSpec as P

BR = 4
CAPX = 2


FILTER = 0.055
UNROLL = 6
VMEM_GRANT = 8 * 1024 * 1024


def passed_along(shard, axis, by):
    size = lax.axis_size(axis)
    return lax.ppermute(shard, axis, [(i, (i + by) % size) for i in range(size)])


def window_blocks(slots, places):
    onehot = (places[:, None] == jnp.arange(BR * BR)[None, :]).astype(jnp.float32)
    return jnp.einsum("qp,qxy->pxy", onehot, slots, precision=lax.Precision.HIGHEST)


def block_norms(blocks):
    return jnp.sqrt(jnp.sum(blocks * blocks, axis=(-2, -1)))


def stop_product(density_panel, panel_labels, panel_norms, ks_slots, ks_places, targets, half_cols):
    block_size = density_panel.shape[-1]
    limit = FILTER * block_size * math.sqrt(block_size)
    window = window_blocks(ks_slots, ks_places)
    window_norms = block_norms(window)
    target_rows = targets // half_cols
    target_cols = targets % half_cols
    slot_range = jnp.arange(density_panel.shape[0])
    inner_rows = jnp.arange(BR)
    matches = (panel_labels[None, None, :, 0] == inner_rows[None, :, None]) & (
        panel_labels[None, None, :, 1] == target_cols[:, None, None]
    )
    present_pair = jnp.any(matches, axis=2)
    where_slot = jnp.sum(matches.astype(jnp.int32) * slot_range[None, None, :], axis=2)
    chosen = density_panel[where_slot]
    chosen_norms = panel_norms[where_slot]
    picked = target_rows[:, None] * BR + inner_rows[None, :]
    ks_norms = window_norms[picked]
    retained = present_pair & (ks_norms * chosen_norms >= limit)
    masked = jnp.where(retained[..., None, None], window[picked], 0.0)
    return jnp.einsum("tkxy,tkyz->txz", masked, chosen, precision=lax.Precision.HIGHEST)


def panel_plan(d_blocks, d_index, row_perm, ks_blocks, ks_index, c_index):
    row_count = lax.axis_size("row")
    block_size = d_blocks.shape[-1]
    blocks = d_blocks.reshape(-1, block_size, block_size)
    slot_list = d_index.reshape(-1, 2)
    block_rows = row_perm.shape[0]
    half_cols = block_rows // lax.axis_size("col")
    capacity = 3 * row_count // 2
    position = jnp.sum(
        jnp.where(slot_list[:, 0:1] == jnp.arange(block_rows)[None, :], row_perm[None, :], 0),
        axis=1,
    )
    grid_panel = position // BR
    inner_row = position % BR
    onehot = (grid_panel[:, None] == jnp.arange(row_count)[None, :]).astype(jnp.int32)
    arrival_rank = jnp.sum((jnp.cumsum(onehot, axis=0) - onehot) * onehot, axis=1)
    send_slot = grid_panel * CAPX + arrival_rank
    outgoing = (
        jnp.zeros((row_count * CAPX, block_size, block_size), jnp.float32).at[send_slot].set(blocks)
    )
    outgoing = outgoing.reshape(row_count, CAPX, block_size, block_size)
    labels = (
        jnp.full((row_count * CAPX, 2), -1, jnp.int32)
        .at[send_slot]
        .set(jnp.stack([inner_row, slot_list[:, 1]], axis=1))
    )
    labels = labels.reshape(row_count, CAPX, 2)
    arrived, arrived_labels = (
        lax.all_to_all(outgoing, "row", split_axis=0, concat_axis=0, tiled=True),
        lax.all_to_all(labels, "row", split_axis=0, concat_axis=0, tiled=True),
    )
    arrived = arrived.reshape(-1, block_size, block_size)
    arrived_labels = arrived_labels.reshape(-1, 2)
    keep_order = jnp.argsort((arrived_labels[:, 0] < 0).astype(jnp.int32), stable=True)[:capacity]
    density_panel = arrived[keep_order]
    panel_labels = arrived_labels[keep_order]
    ks_all, ks_places = (
        lax.all_gather(ks_blocks, "col", axis=1, tiled=True),
        lax.all_gather(ks_index, "col", axis=1, tiled=True),
    )
    ks_all = ks_all[0]
    ks_places = ks_places[0]
    targets = c_index.reshape(-1)
    stop_count = ks_all.shape[0]
    panel_norms = block_norms(density_panel)
    accumulated = jnp.zeros((targets.shape[0], block_size, block_size), jnp.float32)
    for station in range(stop_count):
        accumulated = accumulated + stop_product(
            density_panel,
            panel_labels,
            panel_norms,
            ks_all[station],
            ks_places[station],
            targets,
            half_cols,
        )
        if station + 1 < stop_count:
            density_panel, panel_labels, panel_norms = passed_along(
                (density_panel, panel_labels, panel_norms), "row", -1
            )
    return accumulated.reshape(c_index.shape + (block_size, block_size))


def ring_order(count):
    return list(range(0, count, 2)) + list(range(1, count, 2))[::-1]


def split_bf16(x):
    high = x.astype(jnp.bfloat16)
    return high, (x - high.astype(jnp.float32)).astype(jnp.bfloat16)


def norm_of(x):
    columns = jnp.sum(x * x, axis=0, keepdims=True)
    return jnp.sqrt(jnp.sum(columns, axis=1, keepdims=True))


def in_vmem(x):
    return pltpu.with_memory_space_constraint(x, pltpu.VMEM)


def in_hbm(x):
    return pltpu.with_memory_space_constraint(x, pltpu.HBM)


VMEM_SPEC = pl.BlockSpec(memory_space=pltpu.VMEM)
HBM_SPEC = pl.BlockSpec(memory_space=pltpu.HBM)
GRANT = pltpu.CompilerParams(vmem_limit_bytes=VMEM_GRANT)


def small_cost(microseconds):
    return pl.CostEstimate(flops=0, bytes_accessed=int(3.7e6 * microseconds), transcendentals=0)


def start_all(pairs, sems):
    copies = [pltpu.make_async_copy(src, dst, sems.at[n]) for n, (src, dst) in enumerate(pairs)]
    for copy in copies:
        copy.start()
    return copies


def matrix_of(ref, rows):
    return ref.at[pl.ds(0, rows)].reshape(rows, ref.shape[2])


def pack_kernel(lead, index_ref, blocks_ref, lead_ref, rest_ref, index, sems):
    slots = index.shape[3]
    lead_rows, rest_rows = lead_ref.shape[0] - 1, rest_ref.shape[0] - 1
    copies = start_all(
        [
            (index_ref, index),
            (blocks_ref.at[pl.ds(0, lead_rows)], matrix_of(lead_ref, lead_rows)),
            (blocks_ref.at[pl.ds(lead_rows, rest_rows)], matrix_of(rest_ref, rest_rows)),
        ],
        sems,
    )
    lane = lax.broadcasted_iota(jnp.int32, lead_ref.shape[1:], 1)
    copies[0].wait()
    for ref, rows, first, count in ((lead_ref, lead_rows, 0, lead), (rest_ref, rest_rows, lead, slots - lead)):
        labels = jnp.zeros(ref.shape[1:], jnp.int32)
        for n in range(count):
            for field in range(2):
                labels = jnp.where(lane == 2 * n + field, index[0, 0, field, first + n], labels)
        ref[rows] = labels.astype(jnp.float32)
    for copy in copies[1:]:
        copy.wait()


def pack(blocks, index, lead):
    slots = index.shape[3]
    rows, width = blocks.shape
    lead_rows = rows // slots * lead
    return pl.pallas_call(
        functools.partial(pack_kernel, lead),
        out_shape=(
            pltpu.VMEM((lead_rows + 1, 1, width), jnp.float32),
            pltpu.VMEM((rows - lead_rows + 1, 1, width), jnp.float32),
        ),
        in_specs=[HBM_SPEC] * 2,
        out_specs=(VMEM_SPEC,) * 2,
        scratch_shapes=[pltpu.SMEM(index.shape, jnp.int32), pltpu.SemaphoreType.DMA((3,))],
        compiler_params=GRANT,
        cost_estimate=small_cost(1),
    )(in_hbm(index), in_hbm(blocks))


def field_bits(count):
    return count.bit_length()


def lines_of(entries, lanes):
    return -(-entries // lanes)


def window_kernel(half_cols, *refs):
    hbm_refs, twin_ref = refs[:5], refs[5]
    parts_ref, norms_ref, table_ref = refs[6:9]
    perm, own_place, twin_place, targets, own = refs[9:14]
    stop_at, target_at, table, sems, out_sem = refs[14:]
    slot_bits, target_bits = field_bits(parts_ref.shape[0]), field_bits(targets.shape[2])
    no_slot, no_target = (1 << slot_bits) - 1, (1 << target_bits) - 1
    lanes = table.shape[1]
    column_line = lines_of(perm.shape[0], lanes)
    row, row_count = lax.axis_index("row"), lax.axis_size("row")
    count = own.shape[0]
    _, half_stops, present = own_place.shape
    col = lax.axis_index("col")
    copies = start_all(list(zip(hbm_refs, refs[9:14])), sems)

    def split_half(half, ref):
        def one(q, _):
            block = ref[q]
            parts_ref[half * count + q] = jnp.concatenate(split_bf16(block), axis=1)
            norms_ref[half * count + q] = jnp.broadcast_to(norm_of(block), norms_ref.shape[1:])

        lax.fori_loop(0, count, one, None, unroll=4)

    split_half(1, twin_ref)
    for i in range(stop_at.shape[0]):
        stop_at[i] = no_slot
    for i in range(target_at.shape[0]):
        target_at[i] = no_target
    for copy in copies[:4]:
        copy.wait()
    for local in range(half_stops):
        own_base = (col * half_stops + local) * BR * BR
        twin_base = ((1 - col) * half_stops + local) * BR * BR
        for q in range(present):
            stop_at[own_base + own_place[0, local, q]] = local * present + q
            stop_at[twin_base + twin_place[0, local, q]] = (half_stops + local) * present + q
    for t in range(targets.shape[2]):
        target_at[targets[0, 0, t]] = t
    for j in range(half_cols):
        packed = target_at[j]
        for i in range(1, BR):
            packed = packed | (target_at[i * half_cols + j] << (target_bits * i))
        table[column_line + j // lanes, j % lanes] = packed.astype(jnp.float32)
    for block_row in range(perm.shape[0]):
        behind = lax.div(perm[block_row], BR) - row
        stop = jnp.where(behind < 0, behind + row_count, behind)
        place = jnp.minimum(stop, 2 * half_stops - 1) * BR * BR + lax.rem(perm[block_row], BR)
        packed = stop_at[place]
        for i in range(1, BR):
            packed = packed | (stop_at[place + i * BR] << (slot_bits * i))
        packed = jnp.where(stop < 2 * half_stops, packed, (1 << (slot_bits * BR)) - 1)
        table[block_row // lanes, block_row % lanes] = packed.astype(jnp.float32)
    publish = pltpu.make_async_copy(table, table_ref, out_sem)
    publish.start()
    copies[4].wait()
    split_half(0, own)
    publish.wait()


def prepare_window(row_perm, own_places, twin_places, targets, own, twin, half_cols):
    count, block_size, _ = own.shape
    lines = lines_of(row_perm.shape[0], block_size) + lines_of(half_cols, block_size)
    lines = -(-lines // 8) * 8
    held = [row_perm, own_places, twin_places, targets]
    return pl.pallas_call(
        functools.partial(window_kernel, half_cols),
        out_shape=(
            pltpu.VMEM((2 * count, block_size, 2 * block_size), jnp.bfloat16),
            pltpu.VMEM((2 * count, 1, block_size), jnp.float32),
            pltpu.VMEM((lines, block_size), jnp.float32),
        ),
        in_specs=[HBM_SPEC] * 5 + [VMEM_SPEC],
        out_specs=(VMEM_SPEC,) * 3,
        scratch_shapes=[
            *(pltpu.SMEM(x.shape, jnp.int32) for x in held),
            pltpu.VMEM(own.shape, jnp.float32),
            pltpu.SMEM((2 * own_places.shape[1] * BR * BR,), jnp.int32),
            pltpu.SMEM((BR * half_cols,), jnp.int32),
            pltpu.SMEM((lines, block_size), jnp.float32),
            pltpu.SemaphoreType.DMA((5,)),
            pltpu.SemaphoreType.DMA,
        ],
        compiler_params=GRANT,
        cost_estimate=small_cost(2),
    )(*map(in_hbm, held), in_hbm(own), in_vmem(twin))


def product_kernel(config, *refs):
    block_rows, half_cols, limit, pieces, first, final = config
    table_ref, parts_ref, norms_ref = refs[:3]
    chunk_refs = refs[3 : 3 + len(pieces)]
    rest = refs[3 + len(pieces) + (not first) + (final == "touched") :]
    c_ref = rest[0]
    if final:
        out_ref = rest[1]
        rest = rest[1:]
    listed, touched, held, out_sems = rest[1:]
    block_size = c_ref.shape[-1]
    slot_bits, target_bits = field_bits(parts_ref.shape[0]), field_bits(c_ref.shape[0])
    no_slot, no_target = (1 << slot_bits) - 1, (1 << target_bits) - 1
    code_bits = slot_bits + target_bits

    def target_of(entry):
        return (entry >> slot_bits) & no_target

    if first:
        c_ref[...] = jnp.zeros_like(c_ref)

    lane = lax.broadcasted_iota(jnp.int32, (1, block_size), 1).astype(jnp.float32)
    label_rows = -(-max(pieces) // 8) * 8
    line = lax.broadcasted_iota(jnp.int32, (label_rows, 1), 0).astype(jnp.float32)
    slot_lines = lines_of(block_rows, block_size)
    target_lines = lines_of(half_cols, block_size)

    def look_up(cells, first_line, lines):
        found = 0.0
        for n in range(lines):
            entries = table_ref[pl.ds(first_line + n, 1), :]
            hit = cells - float(n * block_size) == lane
            found += jnp.sum(jnp.where(hit, entries, 0.0), axis=1, keepdims=True)
        return found

    read = []
    for chunk_ref, blocks in zip(chunk_refs, pieces):
        labels = jnp.broadcast_to(chunk_ref[blocks * block_size], (label_rows, block_size))
        block_row, column = (
            jnp.sum(jnp.where(lane == 2.0 * line + float(field), labels, 0.0), axis=1, keepdims=True)
            for field in range(2)
        )
        slot = look_up(block_row, 0, slot_lines).astype(jnp.int32)
        target = look_up(column, slot_lines, target_lines).astype(jnp.int32)
        blocks_ref = matrix_of(chunk_ref, blocks * block_size)
        read += [(blocks_ref, b, slot[b, 0], target[b, 0]) for b in range(blocks)]
    pairs, kept = jnp.int32(0), jnp.int32(0)
    for blocks_ref, b, slots, targets in read:
        before = pairs
        for i in range(BR):
            ks = (slots >> (slot_bits * i)) & no_slot
            target = (targets >> (target_bits * i)) & no_target
            listed[pairs] = ks | (target << slot_bits) | (kept << code_bits)
            pairs = pairs + ((ks != no_slot) & (target != no_target)).astype(jnp.int32)
        held[kept] = blocks_ref[pl.ds(b * block_size, block_size), :]
        kept = kept + (pairs > before).astype(jnp.int32)
    for u in range(UNROLL):
        listed[pairs + u] = 0

    def multiply(step, _):
        for u in range(UNROLL):
            at = step * UNROLL + u
            entry = listed[at]
            ks, target, slot = entry & no_slot, target_of(entry), entry >> code_bits
            density = held[slot]
            bound = jnp.where(at < pairs, limit, jnp.inf)
            keep = norms_ref[ks] * norm_of(density) >= bound
            high, low = split_bf16(density)
            weights = jnp.concatenate(
                [
                    jnp.concatenate([high, low], axis=1),
                    jnp.concatenate([high, jnp.zeros_like(low)], axis=1),
                ],
                axis=0,
            )
            both = jnp.dot(parts_ref[ks], weights, preferred_element_type=jnp.float32)
            value = both[:, :block_size] + both[:, block_size:]
            c_ref[target] += jnp.where(keep, value, 0.0)

    lax.fori_loop(0, lax.div(pairs + UNROLL - 1, UNROLL), multiply, None)
    if final == "whole":
        copy = pltpu.make_async_copy(c_ref, out_ref, out_sems.at[0])
        copy.start()
        copy.wait()
    elif final == "touched":
        targets = c_ref.shape[0]
        for t in range(targets):
            touched[t] = 0

        def each_target(act, before, after):
            def one(p, _):
                target = target_of(listed[p])

                @pl.when(touched[target] == before)
                def _():
                    act(pltpu.make_async_copy(c_ref.at[target], out_ref.at[target], out_sems.at[target]))
                    touched[target] = after

            lax.fori_loop(0, pairs, one, None)

        each_target(lambda copy: copy.start(), 0, 1)
        each_target(lambda copy: copy.wait(), 1, 2)


def add_products(sizes, window, accumulated, group, shape, final=None, written=None):
    block_size = shape[-1]
    limit = FILTER * block_size * math.sqrt(block_size)
    first = accumulated is None
    pieces = [count for count, _ in group]
    chunks = [chunk for _, chunk in group]
    blocks = sum(pieces)
    parts, norms, table = window
    operands = [*map(in_vmem, (table, parts, norms, *chunks))]
    aliases = {}
    if not first:
        aliases = {len(operands): 0}
        operands.append(in_vmem(accumulated))
    if written is not None:
        aliases[len(operands)] = 1
        operands.append(in_hbm(written))
    in_specs = [VMEM_SPEC] * (len(operands) - (written is not None)) + [HBM_SPEC] * (written is not None)
    longest = blocks * BR + 2 * UNROLL
    outs = 1 if final is None else 2
    out_shape = [pltpu.VMEM(shape, jnp.float32), pltpu.HBM(shape, jnp.float32)][:outs]
    return pl.pallas_call(
        functools.partial(product_kernel, (*sizes, limit, pieces, first, final)),
        out_shape=out_shape,
        in_specs=in_specs,
        out_specs=[VMEM_SPEC, HBM_SPEC][:outs],
        scratch_shapes=[
            pltpu.SMEM((longest,), jnp.int32),
            pltpu.SMEM((shape[0],), jnp.int32),
            pltpu.VMEM((blocks, block_size, block_size), jnp.float32),
            pltpu.SemaphoreType.DMA((shape[0],)),
        ],
        input_output_aliases=aliases,
        compiler_params=GRANT,
        cost_estimate=small_cost(2),
    )(*operands)


def tied(values, token):
    return lax.optimization_barrier((*values, token))[:-1]


def ring_plan(d_blocks, d_index, row_perm, ks_blocks, ks_index, c_index):
    row_count = lax.axis_size("row")
    block_size = d_blocks.shape[-1]
    half_cols = row_perm.shape[0] // lax.axis_size("col")
    slots = d_blocks.shape[2]
    lead = slots // 2
    order = ring_order(row_count)
    forward = [(order[i], order[(i + 1) % row_count]) for i in range(row_count)]
    backward = [(b, a) for a, b in forward]
    twins = [(0, 1), (1, 0)]
    shape = (c_index.shape[-1], block_size, block_size)
    sizes = (row_perm.shape[0], half_cols)

    a_fwd, b_fwd = pack(d_blocks.reshape(-1, block_size), jnp.swapaxes(d_index, 2, 3), lead)
    a_bwd, b_bwd = a_fwd, b_fwd
    ks_own = ks_blocks.reshape(-1, block_size, block_size)
    ks_twin = lax.ppermute(ks_own, "col", twins)
    places_twin = lax.ppermute(ks_index, "col", twins)
    window = prepare_window(row_perm, ks_index, places_twin, c_index, ks_own, ks_twin, half_cols)
    accumulated, written = None, []
    group = [(lead, a_fwd), (slots - lead, b_bwd)]
    half = row_count // 2
    for step in range(1, half + 1):
        a_fwd = lax.ppermute(a_fwd, "row", forward)
        b_bwd = lax.ppermute(b_bwd, "row", backward)
        if step > 1:
            final = {half - 1: "whole", half: "touched"}.get(step)
            if step == half - 1:
                (accumulated,) = tied((accumulated,), a_fwd)
                group += [(lead, a_fwd), (slots - lead, b_bwd)]
            accumulated, *written = add_products(sizes, window, accumulated, group, shape, final, *written)
            group = []
        if step < half:
            if step > 1:
                token = window[1] if step == 2 else before
                (a_bwd,) = tied((a_bwd,), token)
                (b_fwd,) = tied((b_fwd,), token)
            before = accumulated
            a_bwd = lax.ppermute(a_bwd, "row", backward)
            b_fwd = lax.ppermute(b_fwd, "row", forward)
            if step < half - 1:
                group += [(lead, a_fwd), (slots - lead, b_bwd)]
            group += [(lead, a_bwd), (slots - lead, b_fwd)]
    for group in ([(lead, a_fwd)], [(slots - lead, b_bwd)]):
        accumulated, *written = add_products(sizes, window, accumulated, group, shape, "touched", *written)
    return written[0].reshape(c_index.shape + (block_size, block_size))


def on_device(d_blocks, d_index, row_perm, ks_blocks, ks_index, c_index):
    rows, slots = lax.axis_size("row"), d_blocks.shape[2]
    gathered = rows * slots
    routed = rows * CAPX + 3 * (3 * rows // 2)
    window_slots = lax.axis_size("col") * ks_index.shape[1] * ks_index.shape[2]
    packable = BR * max(field_bits(window_slots), field_bits(c_index.shape[2])) <= 24
    plan = ring_plan if gathered <= routed and packable else panel_plan
    return plan(d_blocks, d_index, row_perm, ks_blocks, ks_index, c_index)


def solution(mesh):
    return jax.shard_map(
        on_device,
        mesh=mesh,
        in_specs=(
            P(("groups", "row"), "col", None, None, None),
            P(("groups", "row"), "col", None, None),
            P("groups"),
            P(("groups", "row"), "col", None, None, None),
            P(("groups", "row"), "col", None),
            P(("groups", "row"), "col", None),
        ),
        out_specs=P(("groups", "row"), "col", None, None, None),
        check_vma=False,
    )
```

```python
import functools
import math

import jax
import jax.numpy as jnp
from jax import lax
from jax.experimental import pallas as pl
from jax.experimental.pallas import tpu as pltpu
from jax.sharding import PartitionSpec as P

BR = 4
CAPX = 2


FILTER = 0.055
UNROLL = 6
VMEM_GRANT = 8 * 1024 * 1024


def passed_along(shard, axis, by):
    size = lax.axis_size(axis)
    return lax.ppermute(shard, axis, [(i, (i + by) % size) for i in range(size)])


def window_blocks(slots, places):
    onehot = (places[:, None] == jnp.arange(BR * BR)[None, :]).astype(jnp.float32)
    return jnp.einsum("qp,qxy->pxy", onehot, slots, precision=lax.Precision.HIGHEST)


def block_norms(blocks):
    return jnp.sqrt(jnp.sum(blocks * blocks, axis=(-2, -1)))


def stop_product(density_panel, panel_labels, panel_norms, ks_slots, ks_places, targets, half_cols):
    block_size = density_panel.shape[-1]
    limit = FILTER * block_size * math.sqrt(block_size)
    window = window_blocks(ks_slots, ks_places)
    window_norms = block_norms(window)
    target_rows = targets // half_cols
    target_cols = targets % half_cols
    slot_range = jnp.arange(density_panel.shape[0])
    inner_rows = jnp.arange(BR)
    matches = (panel_labels[None, None, :, 0] == inner_rows[None, :, None]) & (
        panel_labels[None, None, :, 1] == target_cols[:, None, None]
    )
    present_pair = jnp.any(matches, axis=2)
    where_slot = jnp.sum(matches.astype(jnp.int32) * slot_range[None, None, :], axis=2)
    chosen = density_panel[where_slot]
    chosen_norms = panel_norms[where_slot]
    picked = target_rows[:, None] * BR + inner_rows[None, :]
    ks_norms = window_norms[picked]
    retained = present_pair & (ks_norms * chosen_norms >= limit)
    masked = jnp.where(retained[..., None, None], window[picked], 0.0)
    return jnp.einsum("tkxy,tkyz->txz", masked, chosen, precision=lax.Precision.HIGHEST)


def panel_plan(d_blocks, d_index, row_perm, ks_blocks, ks_index, c_index):
    row_count = lax.axis_size("row")
    block_size = d_blocks.shape[-1]
    blocks = d_blocks.reshape(-1, block_size, block_size)
    slot_list = d_index.reshape(-1, 2)
    block_rows = row_perm.shape[0]
    half_cols = block_rows // lax.axis_size("col")
    capacity = 3 * row_count // 2
    position = jnp.sum(
        jnp.where(slot_list[:, 0:1] == jnp.arange(block_rows)[None, :], row_perm[None, :], 0),
        axis=1,
    )
    grid_panel = position // BR
    inner_row = position % BR
    onehot = (grid_panel[:, None] == jnp.arange(row_count)[None, :]).astype(jnp.int32)
    arrival_rank = jnp.sum((jnp.cumsum(onehot, axis=0) - onehot) * onehot, axis=1)
    send_slot = grid_panel * CAPX + arrival_rank
    outgoing = (
        jnp.zeros((row_count * CAPX, block_size, block_size), jnp.float32).at[send_slot].set(blocks)
    )
    outgoing = outgoing.reshape(row_count, CAPX, block_size, block_size)
    labels = (
        jnp.full((row_count * CAPX, 2), -1, jnp.int32)
        .at[send_slot]
        .set(jnp.stack([inner_row, slot_list[:, 1]], axis=1))
    )
    labels = labels.reshape(row_count, CAPX, 2)
    arrived, arrived_labels = (
        lax.all_to_all(outgoing, "row", split_axis=0, concat_axis=0, tiled=True),
        lax.all_to_all(labels, "row", split_axis=0, concat_axis=0, tiled=True),
    )
    arrived = arrived.reshape(-1, block_size, block_size)
    arrived_labels = arrived_labels.reshape(-1, 2)
    keep_order = jnp.argsort((arrived_labels[:, 0] < 0).astype(jnp.int32), stable=True)[:capacity]
    density_panel = arrived[keep_order]
    panel_labels = arrived_labels[keep_order]
    ks_all, ks_places = (
        lax.all_gather(ks_blocks, "col", axis=1, tiled=True),
        lax.all_gather(ks_index, "col", axis=1, tiled=True),
    )
    ks_all = ks_all[0]
    ks_places = ks_places[0]
    targets = c_index.reshape(-1)
    stop_count = ks_all.shape[0]
    panel_norms = block_norms(density_panel)
    accumulated = jnp.zeros((targets.shape[0], block_size, block_size), jnp.float32)
    for station in range(stop_count):
        accumulated = accumulated + stop_product(
            density_panel,
            panel_labels,
            panel_norms,
            ks_all[station],
            ks_places[station],
            targets,
            half_cols,
        )
        if station + 1 < stop_count:
            density_panel, panel_labels, panel_norms = passed_along(
                (density_panel, panel_labels, panel_norms), "row", -1
            )
    return accumulated.reshape(c_index.shape + (block_size, block_size))


def ring_order(count):
    return list(range(0, count, 2)) + list(range(1, count, 2))[::-1]


def split_bf16(x):
    high = x.astype(jnp.bfloat16)
    return high, (x - high.astype(jnp.float32)).astype(jnp.bfloat16)


def norm_of(x):
    columns = jnp.sum(x * x, axis=0, keepdims=True)
    return jnp.sqrt(jnp.sum(columns, axis=1, keepdims=True))


def in_vmem(x):
    return pltpu.with_memory_space_constraint(x, pltpu.VMEM)


def in_hbm(x):
    return pltpu.with_memory_space_constraint(x, pltpu.HBM)


VMEM_SPEC = pl.BlockSpec(memory_space=pltpu.VMEM)
HBM_SPEC = pl.BlockSpec(memory_space=pltpu.HBM)
GRANT = pltpu.CompilerParams(vmem_limit_bytes=VMEM_GRANT)


def start_all(pairs, sems):
    copies = [pltpu.make_async_copy(src, dst, sems.at[n]) for n, (src, dst) in enumerate(pairs)]
    for copy in copies:
        copy.start()
    return copies


def matrix_of(ref, rows):
    return ref.at[pl.ds(0, rows)].reshape(rows, ref.shape[2])


def pack_kernel(lead, index_ref, blocks_ref, lead_ref, rest_ref, index, sems):
    slots = index.shape[3]
    lead_rows, rest_rows = lead_ref.shape[0] - 1, rest_ref.shape[0] - 1
    copies = start_all(
        [
            (index_ref, index),
            (blocks_ref.at[pl.ds(0, lead_rows)], matrix_of(lead_ref, lead_rows)),
            (blocks_ref.at[pl.ds(lead_rows, rest_rows)], matrix_of(rest_ref, rest_rows)),
        ],
        sems,
    )
    lane = lax.broadcasted_iota(jnp.int32, lead_ref.shape[1:], 1)
    copies[0].wait()
    for ref, rows, first, count in ((lead_ref, lead_rows, 0, lead), (rest_ref, rest_rows, lead, slots - lead)):
        labels = jnp.zeros(ref.shape[1:], jnp.int32)
        for n in range(count):
            for field in range(2):
                labels = jnp.where(lane == 2 * n + field, index[0, 0, field, first + n], labels)
        ref[rows] = labels.astype(jnp.float32)
    for copy in copies[1:]:
        copy.wait()


def pack(blocks, index, lead):
    slots = index.shape[3]
    rows, width = blocks.shape
    lead_rows = rows // slots * lead
    return pl.pallas_call(
        functools.partial(pack_kernel, lead),
        out_shape=(
            pltpu.VMEM((lead_rows + 1, 1, width), jnp.float32),
            pltpu.VMEM((rows - lead_rows + 1, 1, width), jnp.float32),
        ),
        in_specs=[HBM_SPEC] * 2,
        out_specs=(VMEM_SPEC,) * 2,
        scratch_shapes=[pltpu.SMEM(index.shape, jnp.int32), pltpu.SemaphoreType.DMA((3,))],
        compiler_params=GRANT,
    )(in_hbm(index), in_hbm(blocks))


def field_bits(count):
    return count.bit_length()


def lines_of(entries, lanes):
    return -(-entries // lanes)


def window_kernel(half_cols, *refs):
    hbm_refs, twin_ref = refs[:5], refs[5]
    parts_ref, norms_ref, table_ref = refs[6:9]
    perm, own_place, twin_place, targets, own = refs[9:14]
    stop_at, target_at, table, sems, out_sem = refs[14:]
    slot_bits, target_bits = field_bits(parts_ref.shape[0]), field_bits(targets.shape[2])
    no_slot, no_target = (1 << slot_bits) - 1, (1 << target_bits) - 1
    lanes = table.shape[1]
    column_line = lines_of(perm.shape[0], lanes)
    row, row_count = lax.axis_index("row"), lax.axis_size("row")
    count = own.shape[0]
    _, half_stops, present = own_place.shape
    col = lax.axis_index("col")
    copies = start_all(list(zip(hbm_refs, refs[9:14])), sems)

    def split_half(half, ref):
        def one(q, _):
            block = ref[q]
            parts_ref[half * count + q] = jnp.concatenate(split_bf16(block), axis=1)
            norms_ref[half * count + q] = jnp.broadcast_to(norm_of(block), norms_ref.shape[1:])

        lax.fori_loop(0, count, one, None, unroll=4)

    split_half(1, twin_ref)
    for i in range(stop_at.shape[0]):
        stop_at[i] = no_slot
    for i in range(target_at.shape[0]):
        target_at[i] = no_target
    for copy in copies[:4]:
        copy.wait()
    for local in range(half_stops):
        own_base = (col * half_stops + local) * BR * BR
        twin_base = ((1 - col) * half_stops + local) * BR * BR
        for q in range(present):
            stop_at[own_base + own_place[0, local, q]] = local * present + q
            stop_at[twin_base + twin_place[0, local, q]] = (half_stops + local) * present + q
    for t in range(targets.shape[2]):
        target_at[targets[0, 0, t]] = t
    for j in range(half_cols):
        packed = target_at[j]
        for i in range(1, BR):
            packed = packed | (target_at[i * half_cols + j] << (target_bits * i))
        table[column_line + j // lanes, j % lanes] = packed.astype(jnp.float32)
    for block_row in range(perm.shape[0]):
        behind = lax.div(perm[block_row], BR) - row
        stop = jnp.where(behind < 0, behind + row_count, behind)
        place = jnp.minimum(stop, 2 * half_stops - 1) * BR * BR + lax.rem(perm[block_row], BR)
        packed = stop_at[place]
        for i in range(1, BR):
            packed = packed | (stop_at[place + i * BR] << (slot_bits * i))
        packed = jnp.where(stop < 2 * half_stops, packed, (1 << (slot_bits * BR)) - 1)
        table[block_row // lanes, block_row % lanes] = packed.astype(jnp.float32)
    publish = pltpu.make_async_copy(table, table_ref, out_sem)
    publish.start()
    copies[4].wait()
    split_half(0, own)
    publish.wait()


def prepare_window(row_perm, own_places, twin_places, targets, own, twin, half_cols):
    count, block_size, _ = own.shape
    lines = lines_of(row_perm.shape[0], block_size) + lines_of(half_cols, block_size)
    lines = -(-lines // 8) * 8
    held = [row_perm, own_places, twin_places, targets]
    return pl.pallas_call(
        functools.partial(window_kernel, half_cols),
        out_shape=(
            pltpu.VMEM((2 * count, block_size, 2 * block_size), jnp.bfloat16),
            pltpu.VMEM((2 * count, 1, block_size), jnp.float32),
            pltpu.VMEM((lines, block_size), jnp.float32),
        ),
        in_specs=[HBM_SPEC] * 5 + [VMEM_SPEC],
        out_specs=(VMEM_SPEC,) * 3,
        scratch_shapes=[
            *(pltpu.SMEM(x.shape, jnp.int32) for x in held),
            pltpu.VMEM(own.shape, jnp.float32),
            pltpu.SMEM((2 * own_places.shape[1] * BR * BR,), jnp.int32),
            pltpu.SMEM((BR * half_cols,), jnp.int32),
            pltpu.SMEM((lines, block_size), jnp.float32),
            pltpu.SemaphoreType.DMA((5,)),
            pltpu.SemaphoreType.DMA,
        ],
        compiler_params=GRANT,
    )(*map(in_hbm, held), in_hbm(own), in_vmem(twin))


def product_kernel(config, *refs):
    block_rows, half_cols, limit, pieces, first, final = config
    table_ref, parts_ref, norms_ref = refs[:3]
    chunk_refs = refs[3 : 3 + len(pieces)]
    rest = refs[3 + len(pieces) + (not first) + (final == "touched") :]
    c_ref = rest[0]
    if final:
        out_ref = rest[1]
        rest = rest[1:]
    listed, touched, held, out_sems = rest[1:]
    block_size = c_ref.shape[-1]
    slot_bits, target_bits = field_bits(parts_ref.shape[0]), field_bits(c_ref.shape[0])
    no_slot, no_target = (1 << slot_bits) - 1, (1 << target_bits) - 1
    code_bits = slot_bits + target_bits

    def target_of(entry):
        return (entry >> slot_bits) & no_target

    if first:
        c_ref[...] = jnp.zeros_like(c_ref)

    lane = lax.broadcasted_iota(jnp.int32, (1, block_size), 1).astype(jnp.float32)
    label_rows = -(-max(pieces) // 8) * 8
    line = lax.broadcasted_iota(jnp.int32, (label_rows, 1), 0).astype(jnp.float32)
    slot_lines = lines_of(block_rows, block_size)
    target_lines = lines_of(half_cols, block_size)

    def look_up(cells, first_line, lines):
        found = 0.0
        for n in range(lines):
            entries = table_ref[pl.ds(first_line + n, 1), :]
            hit = cells - float(n * block_size) == lane
            found += jnp.sum(jnp.where(hit, entries, 0.0), axis=1, keepdims=True)
        return found

    read = []
    for chunk_ref, blocks in zip(chunk_refs, pieces):
        labels = jnp.broadcast_to(chunk_ref[blocks * block_size], (label_rows, block_size))
        block_row, column = (
            jnp.sum(jnp.where(lane == 2.0 * line + float(field), labels, 0.0), axis=1, keepdims=True)
            for field in range(2)
        )
        slot = look_up(block_row, 0, slot_lines).astype(jnp.int32)
        target = look_up(column, slot_lines, target_lines).astype(jnp.int32)
        blocks_ref = matrix_of(chunk_ref, blocks * block_size)
        read += [(blocks_ref, b, slot[b, 0], target[b, 0]) for b in range(blocks)]
    pairs, kept = jnp.int32(0), jnp.int32(0)
    for blocks_ref, b, slots, targets in read:
        before = pairs
        for i in range(BR):
            ks = (slots >> (slot_bits * i)) & no_slot
            target = (targets >> (target_bits * i)) & no_target
            listed[pairs] = ks | (target << slot_bits) | (kept << code_bits)
            pairs = pairs + ((ks != no_slot) & (target != no_target)).astype(jnp.int32)
        held[kept] = blocks_ref[pl.ds(b * block_size, block_size), :]
        kept = kept + (pairs > before).astype(jnp.int32)
    for u in range(UNROLL):
        listed[pairs + u] = 0

    def multiply(step, _):
        for u in range(UNROLL):
            at = step * UNROLL + u
            entry = listed[at]
            ks, target, slot = entry & no_slot, target_of(entry), entry >> code_bits
            density = held[slot]
            bound = jnp.where(at < pairs, limit, jnp.inf)
            keep = norms_ref[ks] * norm_of(density) >= bound
            high, low = split_bf16(density)
            weights = jnp.concatenate(
                [
                    jnp.concatenate([high, low], axis=1),
                    jnp.concatenate([high, jnp.zeros_like(low)], axis=1),
                ],
                axis=0,
            )
            both = jnp.dot(parts_ref[ks], weights, preferred_element_type=jnp.float32)
            value = both[:, :block_size] + both[:, block_size:]
            c_ref[target] += jnp.where(keep, value, 0.0)

    lax.fori_loop(0, lax.div(pairs + UNROLL - 1, UNROLL), multiply, None)
    if final == "whole":
        copy = pltpu.make_async_copy(c_ref, out_ref, out_sems.at[0])
        copy.start()
        copy.wait()
    elif final == "touched":
        targets = c_ref.shape[0]
        for t in range(targets):
            touched[t] = 0

        def each_target(act, before, after):
            def one(p, _):
                target = target_of(listed[p])

                @pl.when(touched[target] == before)
                def _():
                    act(pltpu.make_async_copy(c_ref.at[target], out_ref.at[target], out_sems.at[target]))
                    touched[target] = after

            lax.fori_loop(0, pairs, one, None)

        each_target(lambda copy: copy.start(), 0, 1)
        each_target(lambda copy: copy.wait(), 1, 2)


def add_products(sizes, window, accumulated, group, shape, final=None, written=None):
    block_size = shape[-1]
    limit = FILTER * block_size * math.sqrt(block_size)
    first = accumulated is None
    pieces = [count for count, _ in group]
    chunks = [chunk for _, chunk in group]
    blocks = sum(pieces)
    parts, norms, table = window
    operands = [*map(in_vmem, (table, parts, norms, *chunks))]
    aliases = {}
    if not first:
        aliases = {len(operands): 0}
        operands.append(in_vmem(accumulated))
    if written is not None:
        aliases[len(operands)] = 1
        operands.append(in_hbm(written))
    in_specs = [VMEM_SPEC] * (len(operands) - (written is not None)) + [HBM_SPEC] * (written is not None)
    longest = blocks * BR + 2 * UNROLL
    outs = 1 if final is None else 2
    out_shape = [pltpu.VMEM(shape, jnp.float32), pltpu.HBM(shape, jnp.float32)][:outs]
    return pl.pallas_call(
        functools.partial(product_kernel, (*sizes, limit, pieces, first, final)),
        out_shape=out_shape,
        in_specs=in_specs,
        out_specs=[VMEM_SPEC, HBM_SPEC][:outs],
        scratch_shapes=[
            pltpu.SMEM((longest,), jnp.int32),
            pltpu.SMEM((shape[0],), jnp.int32),
            pltpu.VMEM((blocks, block_size, block_size), jnp.float32),
            pltpu.SemaphoreType.DMA((shape[0],)),
        ],
        input_output_aliases=aliases,
        compiler_params=GRANT,
    )(*operands)


def tied(values, token):
    return lax.optimization_barrier((*values, token))[:-1]


def ring_plan(d_blocks, d_index, row_perm, ks_blocks, ks_index, c_index):
    row_count = lax.axis_size("row")
    block_size = d_blocks.shape[-1]
    half_cols = row_perm.shape[0] // lax.axis_size("col")
    slots = d_blocks.shape[2]
    lead = slots // 2
    order = ring_order(row_count)
    forward = [(order[i], order[(i + 1) % row_count]) for i in range(row_count)]
    backward = [(b, a) for a, b in forward]
    twins = [(0, 1), (1, 0)]
    shape = (c_index.shape[-1], block_size, block_size)
    sizes = (row_perm.shape[0], half_cols)

    a_fwd, b_fwd = pack(d_blocks.reshape(-1, block_size), jnp.swapaxes(d_index, 2, 3), lead)
    a_bwd, b_bwd = a_fwd, b_fwd
    ks_own = ks_blocks.reshape(-1, block_size, block_size)
    ks_twin = lax.ppermute(ks_own, "col", twins)
    places_twin = lax.ppermute(ks_index, "col", twins)
    window = prepare_window(row_perm, ks_index, places_twin, c_index, ks_own, ks_twin, half_cols)
    accumulated, written = None, []
    group = [(lead, a_fwd), (slots - lead, b_bwd)]
    half = row_count // 2
    for step in range(1, half + 1):
        a_fwd = lax.ppermute(a_fwd, "row", forward)
        b_bwd = lax.ppermute(b_bwd, "row", backward)
        if step > 1:
            final = {half - 1: "whole", half: "touched"}.get(step)
            if step == half - 1:
                (accumulated,) = tied((accumulated,), a_fwd)
                group += [(lead, a_fwd), (slots - lead, b_bwd)]
            accumulated, *written = add_products(sizes, window, accumulated, group, shape, final, *written)
            group = []
        if step < half:
            if step > 1:
                token = window[1] if step == 2 else before
                (a_bwd,) = tied((a_bwd,), token)
                (b_fwd,) = tied((b_fwd,), token)
            before = accumulated
            a_bwd = lax.ppermute(a_bwd, "row", backward)
            b_fwd = lax.ppermute(b_fwd, "row", forward)
            if step < half - 1:
                group += [(lead, a_fwd), (slots - lead, b_bwd)]
            group += [(lead, a_bwd), (slots - lead, b_fwd)]
    for group in ([(lead, a_fwd)], [(slots - lead, b_bwd)]):
        accumulated, *written = add_products(sizes, window, accumulated, group, shape, "touched", *written)
    return written[0].reshape(c_index.shape + (block_size, block_size))


def on_device(d_blocks, d_index, row_perm, ks_blocks, ks_index, c_index):
    rows, slots = lax.axis_size("row"), d_blocks.shape[2]
    gathered = rows * slots
    routed = rows * CAPX + 3 * (3 * rows // 2)
    window_slots = lax.axis_size("col") * ks_index.shape[1] * ks_index.shape[2]
    packable = BR * max(field_bits(window_slots), field_bits(c_index.shape[2])) <= 24
    plan = ring_plan if gathered <= routed and packable else panel_plan
    return plan(d_blocks, d_index, row_perm, ks_blocks, ks_index, c_index)


def solution(mesh):
    return jax.shard_map(
        on_device,
        mesh=mesh,
        in_specs=(
            P(("groups", "row"), "col", None, None, None),
            P(("groups", "row"), "col", None, None),
            P("groups"),
            P(("groups", "row"), "col", None, None, None),
            P(("groups", "row"), "col", None),
            P(("groups", "row"), "col", None),
        ),
        out_specs=P(("groups", "row"), "col", None, None, None),
        check_vma=False,
    )
```

```python
import functools
import math

import jax
import jax.numpy as jnp
from jax import lax
from jax.experimental import pallas as pl
from jax.experimental.pallas import tpu as pltpu
from jax.sharding import PartitionSpec as P

BR = 4
CAPX = 2


FILTER = 0.055
UNROLL = 6
VMEM_GRANT = 8 * 1024 * 1024


def passed_along(shard, axis, by):
    size = lax.axis_size(axis)
    return lax.ppermute(shard, axis, [(i, (i + by) % size) for i in range(size)])


def window_blocks(slots, places):
    onehot = (places[:, None] == jnp.arange(BR * BR)[None, :]).astype(jnp.float32)
    return jnp.einsum("qp,qxy->pxy", onehot, slots, precision=lax.Precision.HIGHEST)


def block_norms(blocks):
    return jnp.sqrt(jnp.sum(blocks * blocks, axis=(-2, -1)))


def stop_product(density_panel, panel_labels, panel_norms, ks_slots, ks_places, targets, half_cols):
    block_size = density_panel.shape[-1]
    limit = FILTER * block_size * math.sqrt(block_size)
    window = window_blocks(ks_slots, ks_places)
    window_norms = block_norms(window)
    target_rows = targets // half_cols
    target_cols = targets % half_cols
    slot_range = jnp.arange(density_panel.shape[0])
    inner_rows = jnp.arange(BR)
    matches = (panel_labels[None, None, :, 0] == inner_rows[None, :, None]) & (
        panel_labels[None, None, :, 1] == target_cols[:, None, None]
    )
    present_pair = jnp.any(matches, axis=2)
    where_slot = jnp.sum(matches.astype(jnp.int32) * slot_range[None, None, :], axis=2)
    chosen = density_panel[where_slot]
    chosen_norms = panel_norms[where_slot]
    picked = target_rows[:, None] * BR + inner_rows[None, :]
    ks_norms = window_norms[picked]
    retained = present_pair & (ks_norms * chosen_norms >= limit)
    masked = jnp.where(retained[..., None, None], window[picked], 0.0)
    return jnp.einsum("tkxy,tkyz->txz", masked, chosen, precision=lax.Precision.HIGHEST)


def panel_plan(d_blocks, d_index, row_perm, ks_blocks, ks_index, c_index):
    row_count = lax.axis_size("row")
    block_size = d_blocks.shape[-1]
    blocks = d_blocks.reshape(-1, block_size, block_size)
    slot_list = d_index.reshape(-1, 2)
    block_rows = row_perm.shape[0]
    half_cols = block_rows // lax.axis_size("col")
    capacity = 3 * row_count // 2
    position = jnp.sum(
        jnp.where(slot_list[:, 0:1] == jnp.arange(block_rows)[None, :], row_perm[None, :], 0),
        axis=1,
    )
    grid_panel = position // BR
    inner_row = position % BR
    onehot = (grid_panel[:, None] == jnp.arange(row_count)[None, :]).astype(jnp.int32)
    arrival_rank = jnp.sum((jnp.cumsum(onehot, axis=0) - onehot) * onehot, axis=1)
    send_slot = grid_panel * CAPX + arrival_rank
    outgoing = (
        jnp.zeros((row_count * CAPX, block_size, block_size), jnp.float32).at[send_slot].set(blocks)
    )
    outgoing = outgoing.reshape(row_count, CAPX, block_size, block_size)
    labels = (
        jnp.full((row_count * CAPX, 2), -1, jnp.int32)
        .at[send_slot]
        .set(jnp.stack([inner_row, slot_list[:, 1]], axis=1))
    )
    labels = labels.reshape(row_count, CAPX, 2)
    arrived, arrived_labels = (
        lax.all_to_all(outgoing, "row", split_axis=0, concat_axis=0, tiled=True),
        lax.all_to_all(labels, "row", split_axis=0, concat_axis=0, tiled=True),
    )
    arrived = arrived.reshape(-1, block_size, block_size)
    arrived_labels = arrived_labels.reshape(-1, 2)
    keep_order = jnp.argsort((arrived_labels[:, 0] < 0).astype(jnp.int32), stable=True)[:capacity]
    density_panel = arrived[keep_order]
    panel_labels = arrived_labels[keep_order]
    ks_all, ks_places = (
        lax.all_gather(ks_blocks, "col", axis=1, tiled=True),
        lax.all_gather(ks_index, "col", axis=1, tiled=True),
    )
    ks_all = ks_all[0]
    ks_places = ks_places[0]
    targets = c_index.reshape(-1)
    stop_count = ks_all.shape[0]
    panel_norms = block_norms(density_panel)
    accumulated = jnp.zeros((targets.shape[0], block_size, block_size), jnp.float32)
    for station in range(stop_count):
        accumulated = accumulated + stop_product(
            density_panel,
            panel_labels,
            panel_norms,
            ks_all[station],
            ks_places[station],
            targets,
            half_cols,
        )
        if station + 1 < stop_count:
            density_panel, panel_labels, panel_norms = passed_along(
                (density_panel, panel_labels, panel_norms), "row", -1
            )
    return accumulated.reshape(c_index.shape + (block_size, block_size))


def ring_order(count):
    return list(range(0, count, 2)) + list(range(1, count, 2))[::-1]


def split_bf16(x):
    high = x.astype(jnp.bfloat16)
    return high, (x - high.astype(jnp.float32)).astype(jnp.bfloat16)


def norm_of(x):
    columns = jnp.sum(x * x, axis=0, keepdims=True)
    return jnp.sqrt(jnp.sum(columns, axis=1, keepdims=True))


def in_vmem(x):
    return pltpu.with_memory_space_constraint(x, pltpu.VMEM)


def in_hbm(x):
    return pltpu.with_memory_space_constraint(x, pltpu.HBM)


VMEM_SPEC = pl.BlockSpec(memory_space=pltpu.VMEM)
HBM_SPEC = pl.BlockSpec(memory_space=pltpu.HBM)
SMEM_SPEC = pl.BlockSpec(memory_space=pltpu.SMEM)
GRANT = pltpu.CompilerParams(vmem_limit_bytes=VMEM_GRANT)


def start_all(pairs, sems):
    copies = [pltpu.make_async_copy(src, dst, sems.at[n]) for n, (src, dst) in enumerate(pairs)]
    for copy in copies:
        copy.start()
    return copies


def matrix_of(ref, rows):
    return ref.at[pl.ds(0, rows)].reshape(rows, ref.shape[2])


def pack_kernel(index_ref, blocks_ref, lead_ref, rest_ref, index, sems):
    slots = index.shape[3]
    lead_rows, rest_rows = lead_ref.shape[0] - 1, rest_ref.shape[0] - 1
    copies = start_all(
        [
            (index_ref, index),
            (blocks_ref.at[pl.ds(0, lead_rows)], matrix_of(lead_ref, lead_rows)),
            (blocks_ref.at[pl.ds(lead_rows, rest_rows)], matrix_of(rest_ref, rest_rows)),
        ],
        sems,
    )
    lane = lax.broadcasted_iota(jnp.int32, lead_ref.shape[1:], 1)
    copies[0].wait()
    labels = jnp.zeros(lane.shape, jnp.int32)
    for n in range(slots):
        for field in range(2):
            labels = jnp.where(lane == 2 * n + field, index[0, 0, field, n], labels)
    lead_ref[lead_rows] = labels.astype(jnp.float32)
    rest_ref[rest_rows] = labels.astype(jnp.float32)
    for copy in copies[1:]:
        copy.wait()


def pack(blocks, index, lead):
    slots = index.shape[3]
    rows, width = blocks.shape
    lead_rows = rows // slots * lead
    return pl.pallas_call(
        pack_kernel,
        out_shape=(
            pltpu.VMEM((lead_rows + 1, 1, width), jnp.float32),
            pltpu.VMEM((rows - lead_rows + 1, 1, width), jnp.float32),
        ),
        in_specs=[HBM_SPEC] * 2,
        out_specs=(VMEM_SPEC,) * 2,
        scratch_shapes=[pltpu.SMEM(index.shape, jnp.int32), pltpu.SemaphoreType.DMA((3,))],
        compiler_params=GRANT,
    )(in_hbm(index), in_hbm(blocks))


def field_bits(count):
    return count.bit_length()


def lines_of(entries, lanes):
    return -(-entries // lanes)


def window_kernel(half_cols, *refs):
    hbm_refs, twin_ref = refs[:5], refs[5]
    parts_ref, norms_ref, table_ref = refs[6:9]
    perm, own_place, twin_place, targets, own = refs[9:14]
    stop_at, target_at, table, sems, out_sem = refs[14:]
    slot_bits, target_bits = field_bits(parts_ref.shape[0]), field_bits(targets.shape[2])
    no_slot, no_target = (1 << slot_bits) - 1, (1 << target_bits) - 1
    lanes = table.shape[1]
    column_line = lines_of(perm.shape[0], lanes)
    row, row_count = lax.axis_index("row"), lax.axis_size("row")
    count = own.shape[0]
    _, half_stops, present = own_place.shape
    col = lax.axis_index("col")
    copies = start_all(list(zip(hbm_refs, refs[9:14])), sems)

    def split_half(half, ref):
        def one(q, _):
            block = ref[q]
            parts_ref[half * count + q] = jnp.concatenate(split_bf16(block), axis=1)
            norms_ref[half * count + q] = jnp.broadcast_to(norm_of(block), norms_ref.shape[1:])

        lax.fori_loop(0, count, one, None, unroll=4)

    split_half(1, twin_ref)
    for i in range(stop_at.shape[0]):
        stop_at[i] = no_slot
    for i in range(target_at.shape[0]):
        target_at[i] = no_target
    for copy in copies[:4]:
        copy.wait()
    for local in range(half_stops):
        own_base = (col * half_stops + local) * BR * BR
        twin_base = ((1 - col) * half_stops + local) * BR * BR
        for q in range(present):
            stop_at[own_base + own_place[0, local, q]] = local * present + q
            stop_at[twin_base + twin_place[0, local, q]] = (half_stops + local) * present + q
    for t in range(targets.shape[2]):
        target_at[targets[0, 0, t]] = t
    for j in range(half_cols):
        packed = target_at[j]
        for i in range(1, BR):
            packed = packed | (target_at[i * half_cols + j] << (target_bits * i))
        table[column_line + j // lanes, j % lanes] = packed.astype(jnp.float32)
    for block_row in range(perm.shape[0]):
        behind = lax.div(perm[block_row], BR) - row
        stop = jnp.where(behind < 0, behind + row_count, behind)
        place = jnp.minimum(stop, 2 * half_stops - 1) * BR * BR + lax.rem(perm[block_row], BR)
        packed = stop_at[place]
        for i in range(1, BR):
            packed = packed | (stop_at[place + i * BR] << (slot_bits * i))
        packed = jnp.where(stop < 2 * half_stops, packed, (1 << (slot_bits * BR)) - 1)
        table[block_row // lanes, block_row % lanes] = packed.astype(jnp.float32)
    publish = pltpu.make_async_copy(table, table_ref, out_sem)
    publish.start()
    copies[4].wait()
    split_half(0, own)
    publish.wait()


def prepare_window(row_perm, own_places, twin_places, targets, own, twin, half_cols):
    count, block_size, _ = own.shape
    lines = lines_of(row_perm.shape[0], block_size) + lines_of(half_cols, block_size)
    lines = -(-lines // 8) * 8
    held = [row_perm, own_places, twin_places, targets]
    return pl.pallas_call(
        functools.partial(window_kernel, half_cols),
        out_shape=(
            pltpu.VMEM((2 * count, block_size, 2 * block_size), jnp.bfloat16),
            pltpu.VMEM((2 * count, 1, block_size), jnp.float32),
            pltpu.VMEM((lines, block_size), jnp.float32),
        ),
        in_specs=[HBM_SPEC] * 5 + [VMEM_SPEC],
        out_specs=(VMEM_SPEC,) * 3,
        scratch_shapes=[
            *(pltpu.SMEM(x.shape, jnp.int32) for x in held),
            pltpu.VMEM(own.shape, jnp.float32),
            pltpu.SMEM((2 * own_places.shape[1] * BR * BR,), jnp.int32),
            pltpu.SMEM((BR * half_cols,), jnp.int32),
            pltpu.SMEM((lines, block_size), jnp.float32),
            pltpu.SemaphoreType.DMA((5,)),
            pltpu.SemaphoreType.DMA,
        ],
        compiler_params=GRANT,
    )(*map(in_hbm, held), in_hbm(own), in_vmem(twin))


def product_kernel(config, *refs):
    block_rows, half_cols, limit, pieces, first, final, ahead, planned = config
    if planned:
        plan_ref, *refs = refs
    table_ref, parts_ref, norms_ref = refs[:3]
    chunk_refs = refs[3 : 3 + len(pieces)]
    rest = refs[3 + len(pieces) + (not first) + (final == "touched") :]
    c_ref = rest[0]
    if final:
        out_ref = rest[1]
        rest = rest[1:]
    if ahead:
        next_ref = rest[1]
        rest = rest[1:]
    listed, touched, held, out_sems = rest[1:]
    block_size = c_ref.shape[-1]
    slot_bits, target_bits = field_bits(parts_ref.shape[0]), field_bits(c_ref.shape[0])
    no_slot, no_target = (1 << slot_bits) - 1, (1 << target_bits) - 1
    code_bits = slot_bits + target_bits

    def target_of(entry):
        return (entry >> slot_bits) & no_target

    if first:
        c_ref[...] = jnp.zeros_like(c_ref)

    lane = lax.broadcasted_iota(jnp.int32, (1, block_size), 1).astype(jnp.float32)
    label_rows = -(-max(sum(piece) for piece in (*pieces, ahead or (0, 0))) // 8) * 8
    line = lax.broadcasted_iota(jnp.int32, (label_rows, 1), 0).astype(jnp.float32)
    slot_lines = lines_of(block_rows, block_size)
    target_lines = lines_of(half_cols, block_size)

    def look_up(cells, first_line, lines):
        found = 0.0
        for n in range(lines):
            entries = table_ref[pl.ds(first_line + n, 1), :]
            hit = cells - float(n * block_size) == lane
            found += jnp.sum(jnp.where(hit, entries, 0.0), axis=1, keepdims=True)
        return found

    def enlist(at, pairs, slots, targets, block):
        for i in range(BR):
            ks = (slots >> (slot_bits * i)) & no_slot
            target = (targets >> (target_bits * i)) & no_target
            at[pairs] = ks | (target << slot_bits) | (block << code_bits)
            pairs = pairs + ((ks != no_slot) & (target != no_target)).astype(jnp.int32)
        return pairs

    def fill(at, pairs):
        for u in range(UNROLL):
            at[pairs + u] = 0

    if planned:
        listed = plan_ref
        pairs = plan_ref[plan_ref.shape[0] - 1]
        only_block = matrix_of(chunk_refs[0], pieces[0][0] * block_size)

        def density_at(slot):
            return only_block[pl.ds(pl.multiple_of(slot * block_size, block_size), block_size), :]
    else:

        def density_at(slot):
            return held[slot]

        read = []
        for chunk_ref, (blocks, offset) in zip(chunk_refs, pieces):
            labels = jnp.broadcast_to(chunk_ref[blocks * block_size], (label_rows, block_size))
            block_row, column = (
                jnp.sum(jnp.where(lane == 2.0 * line + float(field), labels, 0.0), axis=1, keepdims=True)
                for field in range(2)
            )
            slot = look_up(block_row, 0, slot_lines).astype(jnp.int32)
            target = look_up(column, slot_lines, target_lines).astype(jnp.int32)
            blocks_ref = matrix_of(chunk_ref, blocks * block_size)
            read += [(blocks_ref, b, slot[offset + b, 0], target[offset + b, 0]) for b in range(blocks)]
        if ahead:
            later = [(b, slot[ahead[1] + b, 0], target[ahead[1] + b, 0]) for b in range(ahead[0])]
        pairs, kept = jnp.int32(0), jnp.int32(0)
        for blocks_ref, b, slots, targets in read:
            before = pairs
            pairs = enlist(listed, pairs, slots, targets, kept)
            held[kept] = blocks_ref[pl.ds(b * block_size, block_size), :]
            kept = kept + (pairs > before).astype(jnp.int32)
        fill(listed, pairs)
        if ahead:
            next_pairs = jnp.int32(0)
            for b, slots, targets in later:
                next_pairs = enlist(next_ref, next_pairs, slots, targets, b)
            fill(next_ref, next_pairs)
            next_ref[next_ref.shape[0] - 1] = next_pairs

    def multiply(step, _):
        for u in range(UNROLL):
            at = step * UNROLL + u
            entry = listed[at]
            ks, target, slot = entry & no_slot, target_of(entry), entry >> code_bits
            density = density_at(slot)
            bound = jnp.where(at < pairs, limit, jnp.inf)
            keep = norms_ref[ks] * norm_of(density) >= bound
            high, low = split_bf16(density)
            weights = jnp.concatenate(
                [
                    jnp.concatenate([high, low], axis=1),
                    jnp.concatenate([high, jnp.zeros_like(low)], axis=1),
                ],
                axis=0,
            )
            both = jnp.dot(parts_ref[ks], weights, preferred_element_type=jnp.float32)
            value = both[:, :block_size] + both[:, block_size:]
            c_ref[target] += jnp.where(keep, value, 0.0)

    lax.fori_loop(0, lax.div(pairs + UNROLL - 1, UNROLL), multiply, None)
    if final == "whole":
        copy = pltpu.make_async_copy(c_ref, out_ref, out_sems.at[0])
        copy.start()
        copy.wait()
    elif final == "touched":
        targets = c_ref.shape[0]
        for t in range(targets):
            touched[t] = 0

        def each_target(act, before, after):
            def one(p, _):
                target = target_of(listed[p])

                @pl.when(touched[target] == before)
                def _():
                    act(pltpu.make_async_copy(c_ref.at[target], out_ref.at[target], out_sems.at[target]))
                    touched[target] = after

            lax.fori_loop(0, pairs, one, None)

        each_target(lambda copy: copy.start(), 0, 1)
        each_target(lambda copy: copy.wait(), 1, 2)


def add_products(sizes, window, accumulated, group, shape, final=None, written=None, ahead=None, plan=None):
    block_size = shape[-1]
    limit = FILTER * block_size * math.sqrt(block_size)
    first = accumulated is None
    pieces = [piece[:2] for piece in group]
    chunks = [piece[2] for piece in group]
    blocks = sum(count for count, _ in pieces)
    parts, norms, table = window
    operands = [*map(in_vmem, (table, parts, norms, *chunks))]
    if plan is not None:
        operands.insert(0, pltpu.with_memory_space_constraint(plan, pltpu.SMEM))
    aliases = {}
    if not first:
        aliases = {len(operands): 0}
        operands.append(in_vmem(accumulated))
    if written is not None:
        aliases[len(operands)] = 1
        operands.append(in_hbm(written))
    in_specs = [VMEM_SPEC] * (len(operands) - (written is not None)) + [HBM_SPEC] * (written is not None)
    if plan is not None:
        in_specs[0] = SMEM_SPEC
    longest = blocks * BR + 2 * UNROLL
    outs = 1 if final is None else 2
    out_shape = [pltpu.VMEM(shape, jnp.float32), pltpu.HBM(shape, jnp.float32)][:outs]
    out_specs = [VMEM_SPEC, HBM_SPEC][:outs]
    if ahead:
        out_shape.append(pltpu.SMEM((ahead[0] * BR + 2 * UNROLL,), jnp.int32))
        out_specs.append(SMEM_SPEC)
    return pl.pallas_call(
        functools.partial(
            product_kernel, (*sizes, limit, pieces, first, final, ahead, plan is not None)
        ),
        out_shape=out_shape,
        in_specs=in_specs,
        out_specs=out_specs,
        scratch_shapes=[
            pltpu.SMEM((longest,), jnp.int32),
            pltpu.SMEM((shape[0],), jnp.int32),
            pltpu.VMEM((blocks, block_size, block_size), jnp.float32),
            pltpu.SemaphoreType.DMA((shape[0],)),
        ],
        input_output_aliases=aliases,
        compiler_params=GRANT,
    )(*operands)


def tied(values, token):
    return lax.optimization_barrier((*values, token))[:-1]


def ring_plan(d_blocks, d_index, row_perm, ks_blocks, ks_index, c_index):
    row_count = lax.axis_size("row")
    block_size = d_blocks.shape[-1]
    half_cols = row_perm.shape[0] // lax.axis_size("col")
    slots = d_blocks.shape[2]
    lead = slots // 2
    order = ring_order(row_count)
    forward = [(order[i], order[(i + 1) % row_count]) for i in range(row_count)]
    backward = [(b, a) for a, b in forward]
    twins = [(0, 1), (1, 0)]
    shape = (c_index.shape[-1], block_size, block_size)
    sizes = (row_perm.shape[0], half_cols)

    a_fwd, b_fwd = pack(d_blocks.reshape(-1, block_size), jnp.swapaxes(d_index, 2, 3), lead)
    a_bwd, b_bwd = a_fwd, b_fwd
    ks_own = ks_blocks.reshape(-1, block_size, block_size)
    ks_twin = lax.ppermute(ks_own, "col", twins)
    places_twin = lax.ppermute(ks_index, "col", twins)
    window = prepare_window(row_perm, ks_index, places_twin, c_index, ks_own, ks_twin, half_cols)
    accumulated, written = None, []
    group = [(lead, 0, a_fwd), (slots - lead, lead, b_bwd)]
    half = row_count // 2
    for step in range(1, half + 1):
        a_fwd = lax.ppermute(a_fwd, "row", forward)
        b_bwd = lax.ppermute(b_bwd, "row", backward)
        if step > 1:
            final = {half - 1: "whole", half: "touched"}.get(step)
            if step == half - 1:
                (accumulated,) = tied((accumulated,), a_fwd)
                group += [(lead, 0, a_fwd), (slots - lead, lead, b_bwd)]
            accumulated, *written = add_products(sizes, window, accumulated, group, shape, final, *written)
            group = []
        if step < half:
            if step > 1:
                token = window[1] if step == 2 else before
                (a_bwd,) = tied((a_bwd,), token)
                (b_fwd,) = tied((b_fwd,), token)
            before = accumulated
            a_bwd = lax.ppermute(a_bwd, "row", backward)
            b_fwd = lax.ppermute(b_fwd, "row", forward)
            if step < half - 1:
                group += [(lead, 0, a_fwd), (slots - lead, lead, b_bwd)]
            group += [(lead, 0, a_bwd), (slots - lead, lead, b_fwd)]
    late = (slots - lead, lead)
    accumulated, *written, plan = add_products(
        sizes, window, accumulated, [(lead, 0, a_fwd)], shape, "touched", *written, ahead=late
    )
    _, total = add_products(
        sizes, window, accumulated, [(*late, b_bwd)], shape, "touched", *written, plan=plan
    )
    return total.reshape(c_index.shape + (block_size, block_size))


def on_device(d_blocks, d_index, row_perm, ks_blocks, ks_index, c_index):
    rows, slots = lax.axis_size("row"), d_blocks.shape[2]
    gathered = rows * slots
    routed = rows * CAPX + 3 * (3 * rows // 2)
    window_slots = lax.axis_size("col") * ks_index.shape[1] * ks_index.shape[2]
    packable = BR * max(field_bits(window_slots), field_bits(c_index.shape[2])) <= 24
    plan = ring_plan if gathered <= routed and packable else panel_plan
    return plan(d_blocks, d_index, row_perm, ks_blocks, ks_index, c_index)


def solution(mesh):
    return jax.shard_map(
        on_device,
        mesh=mesh,
        in_specs=(
            P(("groups", "row"), "col", None, None, None),
            P(("groups", "row"), "col", None, None),
            P("groups"),
            P(("groups", "row"), "col", None, None, None),
            P(("groups", "row"), "col", None),
            P(("groups", "row"), "col", None),
        ),
        out_specs=P(("groups", "row"), "col", None, None, None),
        check_vma=False,
    )
```
